32 devices in a mesh: seq: 8 (over y, x, core), tensor: 4 (over z).
Axes of the slice: x: 2, y: 2, z: 4, core: 2. Of those that a mesh axis runs over, the one named last changes fastest.
Arguments:
- weight: bfloat16 [16384, 5376], P(('seq', 'tensor')), may hold values from -2.2 to 2.2
- hidden: bfloat16 [64, 5376], P('seq'), may hold values from -3.2 to 3.2
- targets: int32 [64], replicated, may hold values from 0 to 16383
- branch: int32 [64], replicated, may hold values from 0 to 2
- pair_of_row: int32 [64], replicated, may hold values from 0 to 15, never falling along the last dimension, each value on 1 to 12 neighbouring positions
- ref_log_prob: float32 [64], replicated, may hold values from -20 to -12
- pair_weight: float32 [16], replicated, may hold values from 2 to 16
- token_ids: int32 [6400], P(('seq', 'tensor')), may hold values from 0 to 16383, as said below
- token_grad: bfloat16 [6400, 5376], P(('seq', 'tensor')), may hold values from -0.059814453 to 0.059814453
Outputs:
- dpo_loss: float32 [], replicated
- weight_grad: bfloat16 [16384, 5376], P(('seq', 'tensor'))
- hidden_grad: bfloat16 [64, 5376], P('seq')
The draws below stay inside these ranges and needn't reach their ends.
Inputs may be any that keep to these rules, and one draw needn't show every extreme that they name: `token_ids`: ids of one device's 200 rows fall at most 13 times into the 512 vocabulary rows of any one device; in every draw one such block of vocabulary rows receives exactly 13 ids from every device.
All inputs are finite; a program needn't handle non-finite values.
Results may differ from the reference program's by a relative error of at most 0.007.
Values may be sent and summed in bfloat16 or wider, within the bound.
A program may use at most 128 MiB of HBM per device.

```python
import math
import jax
import jax.numpy as jnp
import numpy as np
from jax import lax

D = 5376
VOCAB_DEV = 512
VOCAB = 16384
RESP = 64
PAIRS = 16
PAIR_MOST = 12
TOK_DEV = 200
TOKENS = 6400
CAP = 13
N_TENSOR = 4
DEVICES = 32


def draw_weight(key, part):
    key = jax.random.fold_in(key, 11)
    noise_key = jax.random.fold_in(key, 0)
    sign_key = jax.random.fold_in(key, 2)
    signs = (2 * jax.random.randint(sign_key, (1, D), 0, 2) - 1).astype(jnp.float32)
    shared = 0.3 * signs
    values = 0.2 * jnp.clip(jax.random.normal(noise_key, (VOCAB, D), jnp.float32), -4.5, 4.5)
    values = values + shared
    return values.astype(jnp.bfloat16)


def draw_hidden(key, part):
    key = jax.random.fold_in(key, 12)
    noise_key = jax.random.fold_in(key, 0)
    values = 0.21 * jnp.clip(jax.random.normal(noise_key, (RESP, D), jnp.float32), -4.5, 4.5)
    return values.astype(jnp.bfloat16)


def draw_token_ids(key, part):
    key = jax.random.fold_in(key, 13)
    hot_key, score_key, offset_key = jax.random.split(key, 3)
    slot_count = DEVICES * CAP
    hot_owner = jax.random.randint(hot_key, (), 0, DEVICES)

    def one_block(block_key):
        score_part, shuffle_part = jax.random.split(block_key)
        slot_index = jnp.arange(slot_count, dtype=jnp.int32)
        scores = jax.random.randint(score_part, (slot_count,), 0, 2 ** 19) * 2048 + slot_index
        scores = jnp.where(slot_index // CAP == hot_owner, -1, scores)
        picked_scores, picked = lax.top_k(scores, TOK_DEV - CAP)
        owners = jnp.concatenate([jnp.full((CAP,), hot_owner, jnp.int32), (picked // CAP).astype(jnp.int32)])
        return jax.random.permutation(shuffle_part, owners)
    owners = jax.vmap(one_block)(jax.random.split(score_key, DEVICES)).reshape(TOKENS)
    return owners * VOCAB_DEV + jax.random.randint(offset_key, (TOKENS,), 0, VOCAB_DEV)


def place_ends(entries, rng, low, high):
    shape = entries.shape
    index_at = [jax.random.randint(jax.random.fold_in(rng, axis), (), 0, shape[axis]) for axis in range(len(shape))]
    entries = entries.at[tuple(index_at)].set(low)
    longest = shape.index(max(shape))
    index_at[longest] = (index_at[longest] + 1) % shape[longest]
    return entries.at[tuple(index_at)].set(high)


def steps_of(stream_key, shape, cuts, smallest, high):
    def one(dim, blocks):
        heights = jax.random.uniform(jax.random.fold_in(jax.random.fold_in(stream_key, 6), dim), (blocks,), jnp.float32, smallest / len(cuts), high / len(cuts))
        return jnp.repeat(jnp.exp(heights), shape[dim] // blocks).reshape((-1,) + (1,) * (len(shape) - dim - 1))

    gain = one(*cuts[0])
    for cut in cuts[1:]:
        gain = gain * one(*cut)
    return gain


def length_profile(count, total, limit, skew):
    portions = [(1 << 20) // math.isqrt(grade ** skew) + 1 for grade in range(2, count + 1)]
    spare, given = total - limit - (count - 1), [1] * (count - 1)
    while spare > 0:
        candidates = [i for i in range(count - 1) if given[i] < limit]
        whole, left = sum([portions[i] for i in candidates]), spare
        for i in candidates:
            extra = min(limit - given[i], max(1, left * portions[i] // whole), spare)
            given[i] = given[i] + extra
            spare = spare - extra
    return np.array([limit] + given)


def uneven_parts(rng, number_of, total, most, slope):
    if number_of == 2:
        one = jax.random.randint(rng, (), max(1, total - most), min(most, total - 1) + 1)
        return jnp.stack([one, total - one])
    tallies = jnp.asarray(length_profile(number_of, total, most, slope), jnp.int32)
    pairs = (number_of - 1) // 2
    donor, taker = tallies[1:1 + 2 * pairs:2], tallies[2:2 + 2 * pairs:2]
    slack = jnp.minimum(donor - 1, most - taker)
    shifted = jax.random.randint(jax.random.fold_in(rng, 1), (pairs,), 0, 1 << 20) % (slack + 1)
    tallies = tallies.at[1:1 + 2 * pairs:2].set(donor - shifted).at[2:2 + 2 * pairs:2].set(taker + shifted)
    return tallies[jax.random.permutation(jax.random.fold_in(rng, 2), number_of)]


def centred(stream_key, dims, width, most, pieces=(), held_as=jnp.bfloat16):
    factor_of = steps_of(stream_key, dims, pieces, -0.22, 0.18) if pieces else 1.0
    values = jax.random.normal(stream_key, dims, jnp.float32) * width * factor_of
    return jnp.minimum(jnp.maximum(values, -most), most).astype(held_as)


def setup_inputs(seed: int = 0) -> dict:
    arg_keys = jax.random.split(jax.random.key(seed), 10)
    return {
        "weight": draw_weight(jax.random.fold_in(arg_keys[9], 71), 0),
        "hidden": draw_hidden(jax.random.fold_in(arg_keys[9], 71), 0),
        "targets": place_ends(jax.random.randint(arg_keys[2], (RESP,), 0, VOCAB), jax.random.fold_in(arg_keys[2], 1), 0, VOCAB - 1).astype(jnp.int32),
        "branch": place_ends(jax.random.randint(arg_keys[3], (RESP,), 0, 3), jax.random.fold_in(arg_keys[3], 1), 0, 2).astype(jnp.int32),
        "pair_of_row": jnp.searchsorted(jnp.cumsum(uneven_parts(arg_keys[4], PAIRS, RESP, PAIR_MOST, 1)), jnp.arange(RESP), side="right").astype(jnp.int32),
        "ref_log_prob": jnp.clip(jax.random.uniform(arg_keys[5], (RESP,), jnp.float32, -20.0, -12.0), -20.0, -12.0),
        "pair_weight": jnp.clip(jnp.exp(jax.random.uniform(arg_keys[6], (PAIRS,), jnp.float32, math.log(2.0), math.log(16.0))), 2.0, 16.0),
        "token_ids": draw_token_ids(jax.random.fold_in(arg_keys[9], 71), 0),
        "token_grad": centred(arg_keys[8], (TOKENS, D), 0.01, 0.059814453, ((0, 32),)),
    }


dpo_beta = 0.1

def reference(weight, hidden, targets, branch, pair_of_row, ref_log_prob, pair_weight, token_ids, token_grad):
    vocab_block = VOCAB_DEV * N_TENSOR
    block_count = VOCAB // vocab_block
    logits = jnp.dot(hidden, weight.T, preferred_element_type=jnp.float32)
    row_top = lax.optimization_barrier(jnp.max(logits, axis=1))
    row_total = lax.optimization_barrier(jnp.sum(jnp.exp(logits - row_top[:, None]), axis=1))
    target_logit = jnp.take_along_axis(logits, targets[:, None].astype(jnp.int32), axis=1)[:, 0]
    log_prob = target_logit - row_top - jnp.log(row_total)
    branch_sign = (branch == 1).astype(jnp.float32) - (branch == 2).astype(jnp.float32)
    member = (pair_of_row[:, None] == jnp.arange(PAIRS, dtype=jnp.int32)[None, :]).astype(jnp.float32)
    margin = lax.optimization_barrier(jnp.sum(member * (branch_sign * (log_prob - ref_log_prob))[:, None], axis=0))
    dpo_loss = jnp.sum(pair_weight * jax.nn.softplus(-dpo_beta * margin))
    push_back = pair_weight * jax.nn.sigmoid(-dpo_beta * margin)
    row_scale = -dpo_beta * branch_sign * lax.optimization_barrier(jnp.sum(member * push_back[None, :], axis=1))
    norm_factor = math.sqrt(D)
    grad_float = token_grad.astype(jnp.float32)
    weight_blocks = weight.reshape(block_count, vocab_block, D)
    logit_blocks = logits.reshape(RESP, block_count, vocab_block).transpose(1, 0, 2)
    block_starts = jnp.arange(block_count, dtype=jnp.int32) * vocab_block
    columns = jnp.arange(vocab_block, dtype=jnp.int32)

    def block_grads(carry, stacked):
        weight_rows, block_logits, begin_row = stacked
        target_hit = (columns[None, :] == (targets - begin_row)[:, None]).astype(jnp.float32)
        probs = jnp.exp(block_logits - row_top[:, None]) / row_total[:, None]
        dlogits = (row_scale[:, None] * (target_hit - probs)).astype(jnp.bfloat16)
        head_grad = jnp.dot(dlogits.T, hidden, preferred_element_type=jnp.float32)
        local_ids = token_ids - begin_row
        inside = (local_ids >= 0) & (local_ids < vocab_block)
        landing = jnp.where(inside, local_ids, vocab_block).astype(jnp.int32)
        embed_grad = jax.ops.segment_sum(grad_float, landing, num_segments=vocab_block + 1)[:vocab_block]
        block_out = (head_grad + norm_factor * embed_grad).astype(jnp.bfloat16)
        return (carry + jnp.dot(dlogits, weight_rows, preferred_element_type=jnp.float32), block_out)
    row_sum, grad_blocks = lax.scan(block_grads, jnp.zeros((RESP, D), jnp.float32), (weight_blocks, logit_blocks, block_starts))
    return (dpo_loss, grad_blocks.reshape(VOCAB, D), row_sum.astype(jnp.bfloat16))
```

```python
import functools
import math

import jax
import jax.numpy as jnp
from jax import lax
from jax.experimental import pallas as pl
from jax.experimental.pallas import tpu as pltpu
from jax.sharding import PartitionSpec as P

dpo_beta = 0.1
LANES = 128
ROWS = 16
CHUNK = 128
MESH = pl.DeviceIdType.MESH
F32, BF16 = jnp.float32, jnp.bfloat16


def pack_plan(capacity, tiles):
    for piece in range(tiles // 2, 0, -1):
        parts = tiles // piece - 1
        if tiles % piece == 0 and (ROWS - capacity) * parts >= capacity:
            return piece, parts
    raise ValueError("no packing")


def exchange_kernel(
    seq, tensor, capacity, piece, parts,
    targets, branch, pair_of_row, ref_log_prob, pair_weight, ids_row, ids_col, hidden, token_grad, weight_hbm,
    arrived, arrived_labels, dlogits, gathered, hidden_grad, loss,
    weight, packed, labels, folded, logits, stat, stats, partial, seq_parts, sums, tensor_parts, done, pieces,
    load_sem, own_sem, send_sems, recv_sems,
):
    n = seq * tensor
    vocab_rows, width = weight.shape
    resp = targets.shape[1]
    tokens = ids_row.shape[1]
    mine_seq, mine_tensor = lax.axis_index("seq"), lax.axis_index("tensor")
    me = mine_seq * tensor + mine_tensor

    def device(rel):
        peer = lax.rem(me + rel, n)
        return (lax.div(peer, tensor), lax.rem(peer, tensor))

    def send(src, dst, kind, target):
        pltpu.make_async_remote_copy(
            src_ref=src, dst_ref=dst, send_sem=send_sems.at[kind], recv_sem=recv_sems.at[kind],
            device_id=target, device_id_type=MESH,
        ).start()

    def wait(sems, kind, ref):
        pltpu.make_async_copy(ref, ref, sems.at[kind]).wait()

    load = pltpu.make_async_copy(weight_hbm, weight, load_sem)
    load.start()
    barrier = pltpu.get_barrier_semaphore()

    def greet(rel, carry):
        pl.semaphore_signal(barrier, inc=1, device_id=device(rel), device_id_type=MESH)
        return carry

    lax.fori_loop(1, n, greet, 0)

    shift = vocab_rows.bit_length() - 1
    owner = jnp.right_shift(ids_row[...], shift)
    owner_col = jnp.right_shift(ids_col[...], shift)
    before = lax.broadcasted_iota(jnp.int32, (tokens, tokens), 0) < lax.broadcasted_iota(
        jnp.int32, (tokens, tokens), 1
    )
    slot = jnp.sum(jnp.where((owner_col == owner) & before, 1.0, 0.0), axis=0, keepdims=True).astype(jnp.int32)
    rel_owner = owner - me
    rel_owner = jnp.where(rel_owner < 0, rel_owner + n, rel_owner)
    spare = jnp.zeros_like(slot)
    for j in range(1, ROWS - capacity):
        spare = spare + jnp.where(slot >= j * parts, 1, 0)
    part_of = slot - spare * parts
    main_row = rel_owner * ROWS + slot
    spare_row = rel_owner * ROWS + capacity + spare
    label = (ids_row[...] - owner * vocab_rows + 1).astype(F32)
    piece_width = piece * LANES

    pl.semaphore_wait(barrier, n - 1)

    mine_rows = pl.ds(pl.multiple_of(mine_seq * ROWS, ROWS), ROWS)
    folded[mine_rows] = hidden[...]
    for k in range(1, seq):
        send(hidden, folded.at[mine_rows], 0, (lax.rem(mine_seq + k, seq), mine_tensor))

    def pack(chunk, carry):
        base = pl.multiple_of(chunk * CHUNK, CHUNK)
        rows = base + lax.broadcasted_iota(jnp.int32, (CHUNK, tokens), 0)
        lane = lax.broadcasted_iota(jnp.int32, (CHUNK, LANES), 1)
        main = rows == main_row
        in_spare = rows == spare_row
        main_pick = jnp.where(main, 1.0, 0.0).astype(BF16)
        tags = jnp.where(lane == 0, jnp.sum(jnp.where(main, label, 0.0), axis=1, keepdims=True), 0.0)
        for part in range(parts):
            last = in_spare & (part_of == part)
            last_pick = jnp.where(last, 1.0, 0.0).astype(BF16)
            tags = jnp.where(
                lane == part + 1, jnp.sum(jnp.where(last, label, 0.0), axis=1, keepdims=True), tags
            )
            here = pl.ds(part * piece_width, piece_width)
            packed[pl.ds(base, CHUNK), here] = (
                jnp.dot(main_pick, token_grad[:, here], preferred_element_type=F32)
                + jnp.dot(
                    last_pick, token_grad[:, parts * piece_width :], preferred_element_type=F32
                )
            ).astype(BF16)
        labels[pl.ds(base, CHUNK), :] = tags

        def send_block(i, inner):
            rel = chunk * (CHUNK // ROWS) + i
            block = pl.ds(pl.multiple_of(rel * ROWS, ROWS), ROWS)

            @pl.when(rel > 0)
            def _():
                send(packed.at[block], arrived.at[block], 1, device(rel))
                send(labels.at[block], arrived_labels.at[block], 2, device(rel))

            return inner

        lax.fori_loop(0, CHUNK // ROWS, send_block, 0)
        return carry

    lax.fori_loop(0, n * ROWS // CHUNK, pack, 0)
    own = pltpu.make_async_copy(packed.at[pl.ds(0, ROWS)], arrived.at[pl.ds(0, ROWS)], own_sem)
    own.start()
    arrived_labels[pl.ds(0, ROWS), :] = labels[pl.ds(0, ROWS), :]

    wait(recv_sems, 0, folded.at[pl.ds(0, (seq - 1) * ROWS)])
    half = width // 2
    for pair in range(seq // 2):
        both = folded[pair * 2 * ROWS : (pair + 1) * 2 * ROWS].astype(F32)
        rows = pl.ds(pair * ROWS, ROWS)
        gathered[rows, :half] = jnp.concatenate([both[0:8], both[16:24]], axis=0).astype(BF16)
        gathered[rows, half:] = jnp.concatenate([both[8:16], both[24:32]], axis=0).astype(BF16)
    load.wait()
    step = 6 * LANES
    logits[...] = jnp.zeros_like(logits)

    def add_logits(i, carry):
        columns = pl.ds(pl.multiple_of(i * step, step), step)
        logits[...] += lax.dot_general(
            weight[:, columns], gathered[:, columns], (((1,), (1,)), ((), ())), preferred_element_type=F32
        )
        return carry

    lax.fori_loop(0, width // step, add_logits, 0)
    value = logits[...]
    top = jnp.max(value, axis=0, keepdims=True)
    hit = lax.broadcasted_iota(jnp.int32, (vocab_rows, resp), 0) == targets[...] - me * vocab_rows
    stat[...] = jnp.concatenate(
        [
            top,
            jnp.sum(jnp.exp(value - top), axis=0, keepdims=True),
            jnp.sum(jnp.where(hit, value, 0.0), axis=0, keepdims=True),
            jnp.zeros((5, resp), F32),
        ],
        axis=0,
    )
    stats[pl.ds(me, 1)] = stat[...][None]

    def send_stat(rel, carry):
        send(stat, stats.at[me], 3, device(rel))
        return carry

    lax.fori_loop(1, n, send_stat, 0)
    wait(recv_sems, 3, stats.at[pl.ds(0, n - 1)])
    tops = stats[:, 0, :]
    row_top = jnp.max(tops, axis=0, keepdims=True)
    row_total = jnp.sum(jnp.exp(tops - row_top) * stats[:, 1, :], axis=0, keepdims=True)
    target_logit = jnp.sum(stats[:, 2, :], axis=0, keepdims=True)
    log_prob = target_logit - row_top - jnp.log(row_total)
    sign = jnp.where(branch[...] == 1, 1.0, 0.0) - jnp.where(branch[...] == 2, 1.0, 0.0)
    pairs = pair_weight.shape[0]
    member = lax.broadcasted_iota(jnp.int32, (pairs, resp), 0) == pair_of_row[...]
    margin = jnp.sum(jnp.where(member, sign * (log_prob - ref_log_prob[...]), 0.0), axis=1, keepdims=True)
    z = -dpo_beta * margin
    softplus = jnp.maximum(z, 0.0) + jnp.log1p(jnp.exp(-jnp.abs(z)))
    loss[...] = jnp.sum(pair_weight[...] * softplus, axis=0, keepdims=True)
    push_back = pair_weight[...] * lax.logistic(z)
    row_scale = -dpo_beta * sign * jnp.sum(jnp.where(member, push_back, 0.0), axis=0, keepdims=True)
    probs = jnp.exp(value - row_top) / row_total
    rounded = (row_scale * (jnp.where(hit, 1.0, 0.0) - probs)).astype(BF16)
    dlogits[...] = rounded
    by_row = jnp.transpose(rounded.astype(F32)).astype(BF16)

    def add_partial(i, carry):
        columns = pl.ds(pl.multiple_of(i * step, step), step)
        partial[:, columns] = jnp.dot(by_row, weight[:, columns], preferred_element_type=F32)
        return carry

    lax.fori_loop(0, width // step, add_partial, 0)
    share = resp // seq
    for k in range(1, seq):
        peer = lax.rem(mine_seq + k, seq)
        rows = pl.ds(pl.multiple_of(peer * share, share), share)
        send(partial.at[rows], seq_parts.at[mine_seq], 4, (peer, mine_tensor))
    rows = pl.ds(pl.multiple_of(mine_seq * share, share), share)
    seq_parts[pl.ds(mine_seq, 1)] = partial[rows, :][None]
    wait(recv_sems, 4, seq_parts.at[pl.ds(0, seq - 1)])
    total = seq_parts[0]
    for k in range(1, seq):
        total = total + seq_parts[k]
    slab = sums.shape[2]
    cuts = [(i, i * slab, min((i + 1) * slab, width)) for i in range(tensor) if i * slab < width]
    sums[...] = jnp.zeros_like(sums)
    for i, low, high in cuts:
        sums[i, :, : high - low] = total[:, low:high]
    for k in range(1, tensor):
        peer = lax.rem(mine_tensor + k, tensor)
        send(sums.at[peer], tensor_parts.at[mine_tensor], 5, (mine_seq, peer))
    tensor_parts[pl.ds(mine_tensor, 1)] = sums[pl.ds(mine_tensor, 1)]
    wait(recv_sems, 5, tensor_parts.at[pl.ds(0, tensor - 1)])
    total = tensor_parts[0]
    for k in range(1, tensor):
        total = total + tensor_parts[k]
    done[...] = total
    pieces[pl.ds(mine_tensor, 1)] = total[None]
    for k in range(1, tensor):
        send(done, pieces.at[mine_tensor], 6, (mine_seq, lax.rem(mine_tensor + k, tensor)))
    wait(recv_sems, 6, pieces.at[pl.ds(0, tensor - 1)])
    for i, low, high in cuts:
        hidden_grad[:, low:high] = pieces[i, :, : high - low].astype(BF16)

    own.wait()
    others = pl.ds(ROWS, (n - 1) * ROWS)
    wait(recv_sems, 2, arrived_labels.at[others])
    wait(recv_sems, 1, arrived.at[others])
    wait(send_sems, 0, folded.at[pl.ds(0, (seq - 1) * ROWS)])
    wait(send_sems, 1, packed.at[others])
    wait(send_sems, 2, labels.at[others])
    wait(send_sems, 3, stats.at[pl.ds(0, n - 1)])
    wait(send_sems, 4, seq_parts.at[pl.ds(0, seq - 1)])
    wait(send_sems, 5, tensor_parts.at[pl.ds(0, tensor - 1)])
    wait(send_sems, 6, pieces.at[pl.ds(0, tensor - 1)])


def weight_grad_kernel(parts, subs, norm, arrived, labels, dlogits, gathered, out, tags, main_pick, rest):
    i = pl.program_id(0)
    vocab_rows, slots = main_pick.shape
    vocab = lax.broadcasted_iota(jnp.int32, (vocab_rows, slots), 0).astype(F32) + 1.0

    @pl.when(i == 0)
    def _():
        tags[...] = jnp.transpose(labels[...])
        main_pick[...] = jnp.where(vocab == tags[0:1, :], 1.0, 0.0).astype(BF16)
        rest[...] = jnp.zeros_like(rest)

    head = jnp.dot(dlogits[...], gathered[...], preferred_element_type=F32)
    sub = lax.rem(i, subs)

    @pl.when(i < parts * subs)
    def _():
        block = arrived[...]
        out[...] = (head + norm * jnp.dot(main_pick[...], block, preferred_element_type=F32)).astype(BF16)
        part = lax.div(i, subs)
        last_pick = jnp.where(vocab == tags[pl.ds(part + 1, 1), :], 1.0, 0.0).astype(BF16)
        rest[pl.ds(sub, 1)] += jnp.dot(last_pick, block, preferred_element_type=F32)[None]

    @pl.when(i >= parts * subs)
    def _():
        out[...] = (head + norm * rest[pl.ds(sub, 1)][0]).astype(BF16)


def shards(
    weight, hidden, targets, branch, pair_of_row, ref_log_prob, pair_weight, token_ids, token_grad
):
    vocab_rows, width = weight.shape
    seq, tensor = lax.axis_size("seq"), lax.axis_size("tensor")
    n = seq * tensor
    resp, tokens, pairs = targets.shape[0], token_ids.shape[0], pair_weight.shape[0]
    capacity = max(2, (2 * tokens + n - 1) // n)
    tiles = width // LANES
    piece, parts = pack_plan(capacity, tiles)
    subs = next(k for k in range(1, piece + 1) if piece % k == 0 and piece // k <= 8)
    block = piece // subs * LANES
    packed_width = parts * piece * LANES
    slab = (tiles + tensor - 1) // tensor * LANES
    half = width // 2
    folded = jnp.concatenate([hidden[:, :half], hidden[:, half:]], axis=0)
    vmem, hbm = pl.BlockSpec(memory_space=pltpu.VMEM), pl.BlockSpec(memory_space=pl.ANY)
    arrived, arrived_labels, dlogits, gathered, hidden_grad, loss = pl.pallas_call(
        functools.partial(exchange_kernel, seq, tensor, capacity, piece, parts),
        out_shape=(
            jax.ShapeDtypeStruct((n * ROWS, packed_width), BF16),
            jax.ShapeDtypeStruct((n * ROWS, LANES), F32),
            jax.ShapeDtypeStruct((vocab_rows, resp), BF16),
            jax.ShapeDtypeStruct((resp, width), BF16),
            jax.ShapeDtypeStruct(hidden.shape, BF16),
            jax.ShapeDtypeStruct((1, 1), F32),
        ),
        in_specs=[vmem] * 9 + [hbm],
        out_specs=(hbm, vmem, vmem, vmem, vmem, vmem),
        scratch_shapes=[
            pltpu.VMEM((vocab_rows, width), BF16),
            pltpu.VMEM((n * ROWS, packed_width), BF16),
            pltpu.VMEM((n * ROWS, LANES), F32),
            pltpu.VMEM((seq * ROWS, half), BF16),
            pltpu.VMEM((vocab_rows, resp), F32),
            pltpu.VMEM((8, resp), F32),
            pltpu.VMEM((n, 8, resp), F32),
            pltpu.VMEM((resp, width), F32),
            pltpu.VMEM((seq, resp // seq, width), F32),
            pltpu.VMEM((tensor, resp // seq, slab), F32),
            pltpu.VMEM((tensor, resp // seq, slab), F32),
            pltpu.VMEM((resp // seq, slab), F32),
            pltpu.VMEM((tensor, resp // seq, slab), F32),
            pltpu.SemaphoreType.DMA,
            pltpu.SemaphoreType.DMA,
            pltpu.SemaphoreType.DMA((7,)),
            pltpu.SemaphoreType.DMA((7,)),
        ],
        compiler_params=pltpu.CompilerParams(
            collective_id=0, has_side_effects=True, vmem_limit_bytes=60 << 20
        ),
        name="exchange",
    )(
        targets.reshape(1, resp),
        branch.reshape(1, resp),
        pair_of_row.reshape(1, resp),
        ref_log_prob.reshape(1, resp),
        pair_weight.reshape(pairs, 1),
        token_ids.reshape(1, tokens),
        token_ids.reshape(tokens, 1),
        folded,
        token_grad,
        weight,
    )
    last = parts * subs - 1
    weight_grad = pl.pallas_call(
        functools.partial(weight_grad_kernel, parts, subs, math.sqrt(width)),
        grid=((parts + 1) * subs,),
        out_shape=jax.ShapeDtypeStruct(weight.shape, BF16),
        in_specs=[
            pl.BlockSpec((n * ROWS, block), lambda i: (0, jnp.minimum(i, last))),
            pl.BlockSpec((n * ROWS, LANES), lambda i: (0, 0)),
            pl.BlockSpec((vocab_rows, resp), lambda i: (0, 0)),
            pl.BlockSpec((resp, block), lambda i: (0, i)),
        ],
        out_specs=pl.BlockSpec((vocab_rows, block), lambda i: (0, i)),
        scratch_shapes=[
            pltpu.VMEM((LANES, n * ROWS), F32),
            pltpu.VMEM((vocab_rows, n * ROWS), BF16),
            pltpu.VMEM((subs, vocab_rows, block), F32),
        ],
        compiler_params=pltpu.CompilerParams(vmem_limit_bytes=56 << 20),
        name="weight_grad",
    )(arrived, arrived_labels, dlogits, gathered)
    return (loss.reshape(()), weight_grad, hidden_grad)


def solution(mesh):
    return jax.shard_map(
        shards,
        mesh=mesh,
        in_specs=(
            P(("seq", "tensor"), None),
            P("seq", None),
            P(),
            P(),
            P(),
            P(),
            P(),
            P(("seq", "tensor")),
            P(("seq", "tensor"), None),
        ),
        out_specs=(P(), P(("seq", "tensor"), None), P("seq", None)),
        check_vma=False,
    )
```

```python
import functools
import math

import jax
import jax.numpy as jnp
from jax import lax
from jax.experimental import pallas as pl
from jax.experimental.pallas import tpu as pltpu
from jax.sharding import PartitionSpec as P

dpo_beta = 0.1
LANES = 128
ROWS = 16
CHUNK = 128
WAVES = 4
MESH = pl.DeviceIdType.MESH
F32, BF16 = jnp.float32, jnp.bfloat16


def pack_plan(capacity, tiles):
    for piece in range(tiles // 2, 0, -1):
        parts = tiles // piece - 1
        if tiles % piece == 0 and (ROWS - capacity) * parts >= capacity:
            return piece, parts
    raise ValueError("no packing")


def exchange_kernel(
    seq, tensor, capacity, piece, parts,
    targets, branch, pair_of_row, ref_log_prob, pair_weight, ids_row, ids_col, hidden, token_grad, weight_hbm,
    arrived, arrived_labels, dlogits, gathered, hidden_grad, loss,
    weight, packed, labels, folded, logits, stat, stats, partial, seq_parts, sums, tensor_parts, done, pieces,
    load_sem, own_sem, send_sems, recv_sems,
):
    n = seq * tensor
    vocab_rows, width = weight.shape
    resp = targets.shape[1]
    tokens = ids_row.shape[1]
    mine_seq, mine_tensor = lax.axis_index("seq"), lax.axis_index("tensor")
    me = mine_seq * tensor + mine_tensor

    def device(rel):
        peer = lax.rem(me + rel, n)
        return (lax.div(peer, tensor), lax.rem(peer, tensor))

    def send(src, dst, kind, target):
        pltpu.make_async_remote_copy(
            src_ref=src, dst_ref=dst, send_sem=send_sems.at[kind], recv_sem=recv_sems.at[kind],
            device_id=target, device_id_type=MESH,
        ).start()

    def wait(sems, kind, ref):
        pltpu.make_async_copy(ref, ref, sems.at[kind]).wait()

    load = pltpu.make_async_copy(weight_hbm, weight, load_sem)
    load.start()
    barrier = pltpu.get_barrier_semaphore()

    def greet(rel, carry):
        pl.semaphore_signal(barrier, inc=1, device_id=device(rel), device_id_type=MESH)
        return carry

    lax.fori_loop(1, n, greet, 0)

    shift = vocab_rows.bit_length() - 1
    owner = jnp.right_shift(ids_row[...], shift)
    owner_col = jnp.right_shift(ids_col[...], shift)
    before = lax.broadcasted_iota(jnp.int32, (tokens, tokens), 0) < lax.broadcasted_iota(
        jnp.int32, (tokens, tokens), 1
    )
    slot = jnp.sum(jnp.where((owner_col == owner) & before, 1.0, 0.0), axis=0, keepdims=True).astype(jnp.int32)
    rel_owner = owner - me
    rel_owner = jnp.where(rel_owner < 0, rel_owner + n, rel_owner)
    spare = jnp.zeros_like(slot)
    for j in range(1, ROWS - capacity):
        spare = spare + jnp.where(slot >= j * parts, 1, 0)
    part_of = slot - spare * parts
    main_row = rel_owner * ROWS + slot
    spare_row = rel_owner * ROWS + capacity + spare
    label = (ids_row[...] - owner * vocab_rows + 1).astype(F32)
    piece_width = piece * LANES

    pl.semaphore_wait(barrier, n - 1)

    mine_rows = pl.ds(pl.multiple_of(mine_seq * ROWS, ROWS), ROWS)
    folded[mine_rows] = hidden[...]
    for k in range(1, seq):
        send(hidden, folded.at[mine_rows], 0, (lax.rem(mine_seq + k, seq), mine_tensor))

    def pack(chunk, carry):
        base = pl.multiple_of(chunk * CHUNK, CHUNK)
        rows = base + lax.broadcasted_iota(jnp.int32, (CHUNK, tokens), 0)
        lane = lax.broadcasted_iota(jnp.int32, (CHUNK, LANES), 1)
        main = rows == main_row
        in_spare = rows == spare_row
        main_pick = jnp.where(main, 1.0, 0.0).astype(BF16)
        tags = jnp.where(lane == 0, jnp.sum(jnp.where(main, label, 0.0), axis=1, keepdims=True), 0.0)
        for part in range(parts):
            last = in_spare & (part_of == part)
            last_pick = jnp.where(last, 1.0, 0.0).astype(BF16)
            tags = jnp.where(
                lane == part + 1, jnp.sum(jnp.where(last, label, 0.0), axis=1, keepdims=True), tags
            )
            here = pl.ds(part * piece_width, piece_width)
            packed[pl.ds(base, CHUNK), here] = (
                jnp.dot(main_pick, token_grad[:, here], preferred_element_type=F32)
                + jnp.dot(
                    last_pick, token_grad[:, parts * piece_width :], preferred_element_type=F32
                )
            ).astype(BF16)
        labels[pl.ds(base, CHUNK), :] = tags

        def send_block(i, inner):
            rel = chunk * (CHUNK // ROWS) + i
            block = pl.ds(pl.multiple_of(rel * ROWS, ROWS), ROWS)

            @pl.when(rel > 0)
            def _():
                send(packed.at[block], arrived.at[block], 1, device(rel))
                send(labels.at[block], arrived_labels.at[block], 2, device(rel))

            return inner

        lax.fori_loop(0, CHUNK // ROWS, send_block, 0)
        return carry

    chunks = n * ROWS // CHUNK

    def send_wave(wave):
        lax.fori_loop(wave * chunks // WAVES, (wave + 1) * chunks // WAVES, pack, 0)

    send_wave(0)
    own = pltpu.make_async_copy(packed.at[pl.ds(0, ROWS)], arrived.at[pl.ds(0, ROWS)], own_sem)
    own.start()
    arrived_labels[pl.ds(0, ROWS), :] = labels[pl.ds(0, ROWS), :]

    wait(recv_sems, 0, folded.at[pl.ds(0, (seq - 1) * ROWS)])
    half = width // 2
    for pair in range(seq // 2):
        both = folded[pair * 2 * ROWS : (pair + 1) * 2 * ROWS].astype(F32)
        rows = pl.ds(pair * ROWS, ROWS)
        gathered[rows, :half] = jnp.concatenate([both[0:8], both[16:24]], axis=0).astype(BF16)
        gathered[rows, half:] = jnp.concatenate([both[8:16], both[24:32]], axis=0).astype(BF16)
    load.wait()
    step = 6 * LANES
    logits[...] = jnp.zeros_like(logits)

    def add_logits(i, carry):
        columns = pl.ds(pl.multiple_of(i * step, step), step)
        logits[...] += lax.dot_general(
            weight[:, columns], gathered[:, columns], (((1,), (1,)), ((), ())), preferred_element_type=F32
        )
        return carry

    lax.fori_loop(0, width // step, add_logits, 0)
    value = logits[...]
    top = jnp.max(value, axis=0, keepdims=True)
    hit = lax.broadcasted_iota(jnp.int32, (vocab_rows, resp), 0) == targets[...] - me * vocab_rows
    stat[...] = jnp.concatenate(
        [
            top,
            jnp.sum(jnp.exp(value - top), axis=0, keepdims=True),
            jnp.sum(jnp.where(hit, value, 0.0), axis=0, keepdims=True),
            jnp.zeros((5, resp), F32),
        ],
        axis=0,
    )
    stats[pl.ds(me, 1)] = stat[...][None]

    def send_stat(rel, carry):
        send(stat, stats.at[me], 3, device(rel))
        return carry

    lax.fori_loop(1, n, send_stat, 0)
    send_wave(1)
    wait(recv_sems, 3, stats.at[pl.ds(0, n - 1)])
    tops = stats[:, 0, :]
    row_top = jnp.max(tops, axis=0, keepdims=True)
    row_total = jnp.sum(jnp.exp(tops - row_top) * stats[:, 1, :], axis=0, keepdims=True)
    target_logit = jnp.sum(stats[:, 2, :], axis=0, keepdims=True)
    log_prob = target_logit - row_top - jnp.log(row_total)
    sign = jnp.where(branch[...] == 1, 1.0, 0.0) - jnp.where(branch[...] == 2, 1.0, 0.0)
    pairs = pair_weight.shape[0]
    member = lax.broadcasted_iota(jnp.int32, (pairs, resp), 0) == pair_of_row[...]
    margin = jnp.sum(jnp.where(member, sign * (log_prob - ref_log_prob[...]), 0.0), axis=1, keepdims=True)
    z = -dpo_beta * margin
    softplus = jnp.maximum(z, 0.0) + jnp.log1p(jnp.exp(-jnp.abs(z)))
    loss[...] = jnp.sum(pair_weight[...] * softplus, axis=0, keepdims=True)
    push_back = pair_weight[...] * lax.logistic(z)
    row_scale = -dpo_beta * sign * jnp.sum(jnp.where(member, push_back, 0.0), axis=0, keepdims=True)
    probs = jnp.exp(value - row_top) / row_total
    rounded = (row_scale * (jnp.where(hit, 1.0, 0.0) - probs)).astype(BF16)
    dlogits[...] = rounded
    by_row = jnp.transpose(rounded.astype(F32)).astype(BF16)

    def add_partial(i, carry):
        columns = pl.ds(pl.multiple_of(i * step, step), step)
        partial[:, columns] = jnp.dot(by_row, weight[:, columns], preferred_element_type=F32)
        return carry

    lax.fori_loop(0, width // step, add_partial, 0)
    share = resp // seq
    for k in range(1, seq):
        peer = lax.rem(mine_seq + k, seq)
        rows = pl.ds(pl.multiple_of(peer * share, share), share)
        send(partial.at[rows], seq_parts.at[mine_seq], 4, (peer, mine_tensor))
    send_wave(2)
    rows = pl.ds(pl.multiple_of(mine_seq * share, share), share)
    seq_parts[pl.ds(mine_seq, 1)] = partial[rows, :][None]
    wait(recv_sems, 4, seq_parts.at[pl.ds(0, seq - 1)])
    total = seq_parts[0]
    for k in range(1, seq):
        total = total + seq_parts[k]
    slab = sums.shape[2]
    cuts = [(i, i * slab, min((i + 1) * slab, width)) for i in range(tensor) if i * slab < width]
    sums[...] = jnp.zeros_like(sums)
    for i, low, high in cuts:
        sums[i, :, : high - low] = total[:, low:high]
    for k in range(1, tensor):
        peer = lax.rem(mine_tensor + k, tensor)
        send(sums.at[peer], tensor_parts.at[mine_tensor], 5, (mine_seq, peer))
    send_wave(3)
    tensor_parts[pl.ds(mine_tensor, 1)] = sums[pl.ds(mine_tensor, 1)]
    wait(recv_sems, 5, tensor_parts.at[pl.ds(0, tensor - 1)])
    total = tensor_parts[0]
    for k in range(1, tensor):
        total = total + tensor_parts[k]
    done[...] = total
    pieces[pl.ds(mine_tensor, 1)] = total[None]
    for k in range(1, tensor):
        send(done, pieces.at[mine_tensor], 6, (mine_seq, lax.rem(mine_tensor + k, tensor)))
    wait(recv_sems, 6, pieces.at[pl.ds(0, tensor - 1)])
    for i, low, high in cuts:
        hidden_grad[:, low:high] = pieces[i, :, : high - low].astype(BF16)

    own.wait()
    others = pl.ds(ROWS, (n - 1) * ROWS)
    wait(recv_sems, 2, arrived_labels.at[others])
    wait(recv_sems, 1, arrived.at[others])
    wait(send_sems, 0, folded.at[pl.ds(0, (seq - 1) * ROWS)])
    wait(send_sems, 1, packed.at[others])
    wait(send_sems, 2, labels.at[others])
    wait(send_sems, 3, stats.at[pl.ds(0, n - 1)])
    wait(send_sems, 4, seq_parts.at[pl.ds(0, seq - 1)])
    wait(send_sems, 5, tensor_parts.at[pl.ds(0, tensor - 1)])
    wait(send_sems, 6, pieces.at[pl.ds(0, tensor - 1)])


def weight_grad_kernel(parts, subs, norm, arrived, labels, dlogits, gathered, out, tags, main_pick, rest):
    i = pl.program_id(0)
    vocab_rows, slots = main_pick.shape
    vocab = lax.broadcasted_iota(jnp.int32, (vocab_rows, slots), 0).astype(F32) + 1.0

    @pl.when(i == 0)
    def _():
        tags[...] = jnp.transpose(labels[...])
        main_pick[...] = jnp.where(vocab == tags[0:1, :], 1.0, 0.0).astype(BF16)
        rest[...] = jnp.zeros_like(rest)

    head = jnp.dot(dlogits[...], gathered[...], preferred_element_type=F32)
    sub = lax.rem(i, subs)

    @pl.when(i < parts * subs)
    def _():
        block = arrived[...]
        out[...] = (head + norm * jnp.dot(main_pick[...], block, preferred_element_type=F32)).astype(BF16)
        part = lax.div(i, subs)
        last_pick = jnp.where(vocab == tags[pl.ds(part + 1, 1), :], 1.0, 0.0).astype(BF16)
        rest[pl.ds(sub, 1)] += jnp.dot(last_pick, block, preferred_element_type=F32)[None]

    @pl.when(i >= parts * subs)
    def _():
        out[...] = (head + norm * rest[pl.ds(sub, 1)][0]).astype(BF16)


def shards(
    weight, hidden, targets, branch, pair_of_row, ref_log_prob, pair_weight, token_ids, token_grad
):
    vocab_rows, width = weight.shape
    seq, tensor = lax.axis_size("seq"), lax.axis_size("tensor")
    n = seq * tensor
    resp, tokens, pairs = targets.shape[0], token_ids.shape[0], pair_weight.shape[0]
    capacity = max(2, (2 * tokens + n - 1) // n)
    tiles = width // LANES
    piece, parts = pack_plan(capacity, tiles)
    subs = next(k for k in range(1, piece + 1) if piece % k == 0 and piece // k <= 8)
    block = piece // subs * LANES
    packed_width = parts * piece * LANES
    slab = (tiles + tensor - 1) // tensor * LANES
    half = width // 2
    folded = jnp.concatenate([hidden[:, :half], hidden[:, half:]], axis=0)
    vmem, hbm = pl.BlockSpec(memory_space=pltpu.VMEM), pl.BlockSpec(memory_space=pl.ANY)
    arrived, arrived_labels, dlogits, gathered, hidden_grad, loss = pl.pallas_call(
        functools.partial(exchange_kernel, seq, tensor, capacity, piece, parts),
        out_shape=(
            jax.ShapeDtypeStruct((n * ROWS, packed_width), BF16),
            jax.ShapeDtypeStruct((n * ROWS, LANES), F32),
            jax.ShapeDtypeStruct((vocab_rows, resp), BF16),
            jax.ShapeDtypeStruct((resp, width), BF16),
            jax.ShapeDtypeStruct(hidden.shape, BF16),
            jax.ShapeDtypeStruct((1, 1), F32),
        ),
        in_specs=[vmem] * 9 + [hbm],
        out_specs=(hbm, vmem, vmem, vmem, vmem, vmem),
        scratch_shapes=[
            pltpu.VMEM((vocab_rows, width), BF16),
            pltpu.VMEM((n * ROWS, packed_width), BF16),
            pltpu.VMEM((n * ROWS, LANES), F32),
            pltpu.VMEM((seq * ROWS, half), BF16),
            pltpu.VMEM((vocab_rows, resp), F32),
            pltpu.VMEM((8, resp), F32),
            pltpu.VMEM((n, 8, resp), F32),
            pltpu.VMEM((resp, width), F32),
            pltpu.VMEM((seq, resp // seq, width), F32),
            pltpu.VMEM((tensor, resp // seq, slab), F32),
            pltpu.VMEM((tensor, resp // seq, slab), F32),
            pltpu.VMEM((resp // seq, slab), F32),
            pltpu.VMEM((tensor, resp // seq, slab), F32),
            pltpu.SemaphoreType.DMA,
            pltpu.SemaphoreType.DMA,
            pltpu.SemaphoreType.DMA((7,)),
            pltpu.SemaphoreType.DMA((7,)),
        ],
        compiler_params=pltpu.CompilerParams(
            collective_id=0, has_side_effects=True, vmem_limit_bytes=60 << 20
        ),
        name="exchange",
    )(
        targets.reshape(1, resp),
        branch.reshape(1, resp),
        pair_of_row.reshape(1, resp),
        ref_log_prob.reshape(1, resp),
        pair_weight.reshape(pairs, 1),
        token_ids.reshape(1, tokens),
        token_ids.reshape(tokens, 1),
        folded,
        token_grad,
        weight,
    )
    last = parts * subs - 1
    weight_grad = pl.pallas_call(
        functools.partial(weight_grad_kernel, parts, subs, math.sqrt(width)),
        grid=((parts + 1) * subs,),
        out_shape=jax.ShapeDtypeStruct(weight.shape, BF16),
        in_specs=[
            pl.BlockSpec((n * ROWS, block), lambda i: (0, jnp.minimum(i, last))),
            pl.BlockSpec((n * ROWS, LANES), lambda i: (0, 0)),
            pl.BlockSpec((vocab_rows, resp), lambda i: (0, 0)),
            pl.BlockSpec((resp, block), lambda i: (0, i)),
        ],
        out_specs=pl.BlockSpec((vocab_rows, block), lambda i: (0, i)),
        scratch_shapes=[
            pltpu.VMEM((LANES, n * ROWS), F32),
            pltpu.VMEM((vocab_rows, n * ROWS), BF16),
            pltpu.VMEM((subs, vocab_rows, block), F32),
        ],
        compiler_params=pltpu.CompilerParams(vmem_limit_bytes=56 << 20),
        name="weight_grad",
    )(arrived, arrived_labels, dlogits, gathered)
    return (loss.reshape(()), weight_grad, hidden_grad)


def solution(mesh):
    return jax.shard_map(
        shards,
        mesh=mesh,
        in_specs=(
            P(("seq", "tensor"), None),
            P("seq", None),
            P(),
            P(),
            P(),
            P(),
            P(),
            P(("seq", "tensor")),
            P(("seq", "tensor"), None),
        ),
        out_specs=(P(), P(("seq", "tensor"), None), P("seq", None)),
        check_vma=False,
    )
```

```python
import functools
import math

import jax
import jax.numpy as jnp
from jax import lax
from jax.experimental import pallas as pl
from jax.experimental.pallas import tpu as pltpu
from jax.sharding import PartitionSpec as P

dpo_beta = 0.1
LANES = 128
ROWS = 16
CHUNK = 128
TOKENS = 7
WAVES = 4
MESH = pl.DeviceIdType.MESH
F32, BF16 = jnp.float32, jnp.bfloat16


def pack_plan(capacity, tiles):
    for piece in range(tiles // 2, 0, -1):
        parts = tiles // piece - 1
        if tiles % piece == 0 and (ROWS - capacity) * parts >= capacity:
            return piece, parts
    raise ValueError("no packing")


def exchange_kernel(
    seq, tensor, capacity, piece, parts, block, early_waves, norm,
    targets, branch, pair_of_row, ref_log_prob, pair_weight, ids_row, ids_col, hidden, token_grad, weight_hbm,
    arrived, base_hbm, tags, dlogits, gathered, hidden_grad, loss,
    weight, packed, folded, logits, stat, stats, partial, seq_parts, sums, tensor_parts, done, pieces,
    load_sem, own_sem, send_sems, recv_sems, *early_scratch,
):
    n = seq * tensor
    vocab_rows, width = weight.shape
    resp = targets.shape[1]
    tokens = ids_row.shape[1]
    mine_seq, mine_tensor = lax.axis_index("seq"), lax.axis_index("tensor")
    me = mine_seq * tensor + mine_tensor

    def device(rel):
        peer = lax.rem(me + rel, n)
        return (lax.div(peer, tensor), lax.rem(peer, tensor))

    def send(src, dst, kind, target):
        pltpu.make_async_remote_copy(
            src_ref=src, dst_ref=dst, send_sem=send_sems.at[kind], recv_sem=recv_sems.at[kind],
            device_id=target, device_id_type=MESH,
        ).start()

    def wait(sems, kind, ref):
        pltpu.make_async_copy(ref, ref, sems.at[kind]).wait()

    load = pltpu.make_async_copy(weight_hbm, weight, load_sem)
    load.start()
    barrier = pltpu.get_barrier_semaphore()

    def greet(rel, carry):
        pl.semaphore_signal(barrier, inc=1, device_id=device(rel), device_id_type=MESH)
        return carry

    lax.fori_loop(1, n, greet, 0)

    shift = vocab_rows.bit_length() - 1
    owner = jnp.right_shift(ids_row[...], shift)
    owner_col = jnp.right_shift(ids_col[...], shift)
    before = lax.broadcasted_iota(jnp.int32, (tokens, tokens), 0) < lax.broadcasted_iota(
        jnp.int32, (tokens, tokens), 1
    )
    slot = jnp.sum(jnp.where((owner_col == owner) & before, 1.0, 0.0), axis=0, keepdims=True).astype(jnp.int32)
    rel_owner = owner - me
    rel_owner = jnp.where(rel_owner < 0, rel_owner + n, rel_owner)
    spare = jnp.zeros_like(slot)
    for j in range(1, ROWS - capacity):
        spare = spare + jnp.where(slot >= j * parts, 1, 0)
    part_of = slot - spare * parts
    main_row = rel_owner * ROWS + slot
    spare_row = rel_owner * ROWS + capacity + spare
    label = (ids_row[...] - owner * vocab_rows + 1).astype(F32)
    piece_width = piece * LANES
    chunks = n * ROWS // CHUNK
    wave_rows = n * ROWS // WAVES
    if early_waves:
        early, base, rest, base_sems = early_scratch

    def exact_dot(left, right, dims):
        high = left.astype(BF16)
        low = (left - high.astype(F32)).astype(BF16)
        ones = right.astype(BF16)
        return lax.dot_general(high, ones, dims, preferred_element_type=F32) + lax.dot_general(
            low, ones, dims, preferred_element_type=F32
        )

    to_rel = lax.broadcasted_iota(jnp.int32, (n, tokens), 0) == rel_owner
    at_slot = jnp.where(lax.broadcasted_iota(jnp.int32, (resp, tokens), 0) == slot, 1.0, 0.0)
    stat[...] = jnp.zeros_like(stat)
    stat[:, 3, :] = exact_dot(jnp.where(to_rel, label, 0.0), at_slot, (((1,), (1,)), ((), ())))

    pl.semaphore_wait(barrier, n - 1)

    mine_rows = pl.ds(pl.multiple_of(mine_seq * ROWS, ROWS), ROWS)
    folded[mine_rows] = hidden[...]
    for k in range(1, seq):
        send(hidden, folded.at[mine_rows], 0, (lax.rem(mine_seq + k, seq), mine_tensor))

    def pack(wave, chunk, carry):
        first = pl.multiple_of(chunk * CHUNK, CHUNK)
        rows = first + lax.broadcasted_iota(jnp.int32, (CHUNK, tokens), 0)
        main = rows == main_row
        in_spare = rows == spare_row
        main_pick = jnp.where(main, 1.0, 0.0).astype(BF16)
        for part in range(parts):
            last = in_spare & (part_of == part)
            last_pick = jnp.where(last, 1.0, 0.0).astype(BF16)
            here = pl.ds(part * piece_width, piece_width)
            packed[pl.ds(first, CHUNK), here] = (
                jnp.dot(main_pick, token_grad[:, here], preferred_element_type=F32)
                + jnp.dot(
                    last_pick, token_grad[:, parts * piece_width :], preferred_element_type=F32
                )
            ).astype(BF16)

        def send_block(i, inner):
            rel = chunk * (CHUNK // ROWS) + i
            src = pl.ds(pl.multiple_of(rel * ROWS, ROWS), ROWS)
            if wave < early_waves:
                land = early.at[src]
            else:
                land = arrived.at[pl.ds(pl.multiple_of(rel * ROWS - early_waves * wave_rows, ROWS), ROWS)]

            @pl.when(rel > 0)
            def _():
                send(packed.at[src], land, TOKENS + wave, device(rel))

            return inner

        lax.fori_loop(0, CHUNK // ROWS, send_block, 0)
        return carry

    def send_wave(wave):
        lax.fori_loop(
            wave * chunks // WAVES, (wave + 1) * chunks // WAVES, functools.partial(pack, wave), 0
        )

    send_wave(0)
    own = pltpu.make_async_copy(
        packed.at[pl.ds(0, ROWS)], (early if early_waves else arrived).at[pl.ds(0, ROWS)], own_sem
    )
    own.start()

    wait(recv_sems, 0, folded.at[pl.ds(0, (seq - 1) * ROWS)])
    half = width // 2
    for pair in range(seq // 2):
        both = folded[pair * 2 * ROWS : (pair + 1) * 2 * ROWS].astype(F32)
        rows = pl.ds(pair * ROWS, ROWS)
        gathered[rows, :half] = jnp.concatenate([both[0:8], both[16:24]], axis=0).astype(BF16)
        gathered[rows, half:] = jnp.concatenate([both[8:16], both[24:32]], axis=0).astype(BF16)
    load.wait()
    step = 6 * LANES
    logits[...] = jnp.zeros_like(logits)

    def add_logits(i, carry):
        columns = pl.ds(pl.multiple_of(i * step, step), step)
        logits[...] += lax.dot_general(
            weight[:, columns], gathered[:, columns], (((1,), (1,)), ((), ())), preferred_element_type=F32
        )
        return carry

    lax.fori_loop(0, width // step, add_logits, 0)
    value = logits[...]
    top = jnp.max(value, axis=0, keepdims=True)
    hit = lax.broadcasted_iota(jnp.int32, (vocab_rows, resp), 0) == targets[...] - me * vocab_rows
    stat[:, 0, :] = jnp.broadcast_to(top, (n, resp))
    stat[:, 1, :] = jnp.broadcast_to(jnp.sum(jnp.exp(value - top), axis=0, keepdims=True), (n, resp))
    stat[:, 2, :] = jnp.broadcast_to(jnp.sum(jnp.where(hit, value, 0.0), axis=0, keepdims=True), (n, resp))
    stats[pl.ds(me, 1)] = stat[pl.ds(0, 1)]

    def send_stat(rel, carry):
        send(stat.at[rel], stats.at[me], 3, device(rel))
        return carry

    lax.fori_loop(1, n, send_stat, 0)
    send_wave(1)
    wait(recv_sems, 3, stats.at[pl.ds(0, n - 1)])
    tops = stats[:, 0, :]
    row_top = jnp.max(tops, axis=0, keepdims=True)
    row_total = jnp.sum(jnp.exp(tops - row_top) * stats[:, 1, :], axis=0, keepdims=True)
    target_logit = jnp.sum(stats[:, 2, :], axis=0, keepdims=True)
    log_prob = target_logit - row_top - jnp.log(row_total)
    sign = jnp.where(branch[...] == 1, 1.0, 0.0) - jnp.where(branch[...] == 2, 1.0, 0.0)
    pairs = pair_weight.shape[0]
    member = lax.broadcasted_iota(jnp.int32, (pairs, resp), 0) == pair_of_row[...]
    margin = jnp.sum(jnp.where(member, sign * (log_prob - ref_log_prob[...]), 0.0), axis=1, keepdims=True)
    z = -dpo_beta * margin
    softplus = jnp.maximum(z, 0.0) + jnp.log1p(jnp.exp(-jnp.abs(z)))
    loss[...] = jnp.sum(pair_weight[...] * softplus, axis=0, keepdims=True)
    push_back = pair_weight[...] * lax.logistic(z)
    row_scale = -dpo_beta * sign * jnp.sum(jnp.where(member, push_back, 0.0), axis=0, keepdims=True)
    probs = jnp.exp(value - row_top) / row_total
    rounded = (row_scale * (jnp.where(hit, 1.0, 0.0) - probs)).astype(BF16)
    dlogits[...] = rounded
    by_row = jnp.transpose(rounded.astype(F32)).astype(BF16)

    def add_partial(i, carry):
        columns = pl.ds(pl.multiple_of(i * step, step), step)
        partial[:, columns] = jnp.dot(by_row, weight[:, columns], preferred_element_type=F32)
        return carry

    lax.fori_loop(0, width // step, add_partial, 0)
    share = resp // seq
    for k in range(1, seq):
        peer = lax.rem(mine_seq + k, seq)
        rows = pl.ds(pl.multiple_of(peer * share, share), share)
        send(partial.at[rows], seq_parts.at[mine_seq], 4, (peer, mine_tensor))
    send_wave(2)
    rows = pl.ds(pl.multiple_of(mine_seq * share, share), share)
    seq_parts[pl.ds(mine_seq, 1)] = partial[rows, :][None]
    wait(recv_sems, 4, seq_parts.at[pl.ds(0, seq - 1)])
    total = seq_parts[0]
    for k in range(1, seq):
        total = total + seq_parts[k]
    slab = sums.shape[2]
    cuts = [(i, i * slab, min((i + 1) * slab, width)) for i in range(tensor) if i * slab < width]
    sums[...] = jnp.zeros_like(sums)
    for i, low, high in cuts:
        sums[i, :, : high - low] = total[:, low:high]
    for k in range(1, tensor):
        peer = lax.rem(mine_tensor + k, tensor)
        send(sums.at[peer], tensor_parts.at[mine_tensor], 5, (mine_seq, peer))
    send_wave(3)
    tensor_parts[pl.ds(mine_tensor, 1)] = sums[pl.ds(mine_tensor, 1)]
    wait(recv_sems, 5, tensor_parts.at[pl.ds(0, tensor - 1)])
    total = tensor_parts[0]
    for k in range(1, tensor):
        total = total + tensor_parts[k]
    done[...] = total
    pieces[pl.ds(mine_tensor, 1)] = total[None]
    for k in range(1, tensor):
        send(done, pieces.at[mine_tensor], 6, (mine_seq, lax.rem(mine_tensor + k, tensor)))
    wait(recv_sems, 6, pieces.at[pl.ds(0, tensor - 1)])
    for i, low, high in cuts:
        hidden_grad[:, low:high] = pieces[i, :, : high - low].astype(BF16)

    slots = n * ROWS
    column = lax.broadcasted_iota(jnp.int32, (resp, slots), 1)
    column = column - jnp.right_shift(column, ROWS.bit_length() - 1) * ROWS
    wanted = lax.broadcasted_iota(jnp.int32, (resp, slots), 0)
    came = lax.broadcasted_iota(jnp.int32, (n, slots), 1)
    came = me - jnp.right_shift(came, ROWS.bit_length() - 1)
    came = jnp.where(came < 0, came + n, came) == lax.broadcasted_iota(jnp.int32, (n, slots), 0)
    sent_labels = stats[:, 3, :]
    tags[...] = jnp.zeros_like(tags)
    for k in range(parts + 1):
        if k == 0:
            chosen = (column == wanted) & (column < capacity)
        else:
            chosen = (column >= capacity) & (wanted == (column - capacity) * parts + (k - 1))
        spread = exact_dot(sent_labels, jnp.where(chosen, 1.0, 0.0), (((1,), (0,)), ((), ())))
        tags[k : k + 1, :] = jnp.sum(jnp.where(came, spread, 0.0), axis=0, keepdims=True)

    own.wait()

    def wait_wave(wave):
        low, high = wave * wave_rows + (ROWS if wave == 0 else 0), (wave + 1) * wave_rows
        wait(send_sems, TOKENS + wave, packed.at[pl.ds(low, high - low)])
        if wave < early_waves:
            wait(recv_sems, TOKENS + wave, early.at[pl.ds(low, high - low)])
        else:
            wait(recv_sems, TOKENS + wave, arrived.at[pl.ds(low - early_waves * wave_rows, high - low)])

    if early_waves:
        for wave in range(early_waves):
            wait_wave(wave)
        count = early_waves * wave_rows
        vocab = lax.broadcasted_iota(jnp.int32, (vocab_rows, count), 0).astype(F32) + 1.0
        main_pick = jnp.where(vocab == tags[0:1, :count], 1.0, 0.0).astype(BF16)
        subs = piece_width // block
        rest[...] = jnp.zeros_like(rest)
        stores = []
        for i in range((parts + 1) * subs):
            here = pl.ds(i * block, block)
            head = jnp.dot(dlogits[...], gathered[:, here], preferred_element_type=F32)
            if i < parts * subs:
                part = i // subs
                last_pick = jnp.where(vocab == tags[part + 1 : part + 2, :count], 1.0, 0.0).astype(BF16)
                base[i] = head + norm * jnp.dot(main_pick, early[:, here], preferred_element_type=F32)
                rest[i % subs] += jnp.dot(last_pick, early[:, here], preferred_element_type=F32)
            else:
                base[i] = head + norm * rest[i % subs]
            stores.append(pltpu.make_async_copy(base.at[i], base_hbm.at[i], base_sems.at[i]))
            stores[-1].start()
        for store in stores:
            store.wait()
    for wave in range(early_waves, WAVES):
        wait_wave(wave)
    wait(send_sems, 0, folded.at[pl.ds(0, (seq - 1) * ROWS)])
    wait(send_sems, 3, stats.at[pl.ds(0, n - 1)])
    wait(send_sems, 4, seq_parts.at[pl.ds(0, seq - 1)])
    wait(send_sems, 5, tensor_parts.at[pl.ds(0, tensor - 1)])
    wait(send_sems, 6, pieces.at[pl.ds(0, tensor - 1)])


def weight_grad_kernel(parts, subs, skipped, norm, arrived, tags, dlogits, gathered, base, out, main_pick, rest):
    i = pl.program_id(0)
    vocab_rows, slots = main_pick.shape
    vocab = lax.broadcasted_iota(jnp.int32, (vocab_rows, slots), 0).astype(F32) + 1.0

    @pl.when(i == 0)
    def _():
        main_pick[...] = jnp.where(vocab == tags[0:1, skipped:], 1.0, 0.0).astype(BF16)
        rest[...] = jnp.zeros_like(rest)

    if skipped:
        before = base[0]
    else:
        before = jnp.dot(dlogits[...], gathered[...], preferred_element_type=F32)
    sub = lax.rem(i, subs)

    @pl.when(i < parts * subs)
    def _():
        block = arrived[...]
        out[...] = (before + norm * jnp.dot(main_pick[...], block, preferred_element_type=F32)).astype(BF16)
        part = lax.div(i, subs)
        last_pick = jnp.where(vocab == tags[pl.ds(part + 1, 1), :][:, skipped:], 1.0, 0.0).astype(BF16)
        rest[pl.ds(sub, 1)] += jnp.dot(last_pick, block, preferred_element_type=F32)[None]

    @pl.when(i >= parts * subs)
    def _():
        out[...] = (before + norm * rest[pl.ds(sub, 1)][0]).astype(BF16)


def shards(
    weight, hidden, targets, branch, pair_of_row, ref_log_prob, pair_weight, token_ids, token_grad
):
    vocab_rows, width = weight.shape
    seq, tensor = lax.axis_size("seq"), lax.axis_size("tensor")
    n = seq * tensor
    resp, tokens, pairs = targets.shape[0], token_ids.shape[0], pair_weight.shape[0]
    capacity = max(2, (2 * tokens + n - 1) // n)
    tiles = width // LANES
    piece, parts = pack_plan(capacity, tiles)
    subs = next(k for k in range(1, piece + 1) if piece % k == 0 and piece // k <= 8)
    block = piece // subs * LANES
    packed_width = parts * piece * LANES
    slab = (tiles + tensor - 1) // tensor * LANES
    half = width // 2
    folded = jnp.concatenate([hidden[:, :half], hidden[:, half:]], axis=0)
    vmem, hbm = pl.BlockSpec(memory_space=pltpu.VMEM), pl.BlockSpec(memory_space=pl.ANY)
    norm = math.sqrt(width)
    slots = n * ROWS
    early_waves = WAVES - 1 if slots * packed_width * 2 <= 8 << 20 else 0
    skipped = early_waves * slots // WAVES
    steps = (parts + 1) * subs
    base_shape = (steps, vocab_rows, block) if early_waves else (1, 8, LANES)
    early_scratch = [
        pltpu.VMEM((skipped, packed_width), BF16),
        pltpu.VMEM(base_shape, F32),
        pltpu.VMEM((subs, vocab_rows, block), F32),
        pltpu.SemaphoreType.DMA((steps,)),
    ]
    arrived, base, tags, dlogits, gathered, hidden_grad, loss = pl.pallas_call(
        functools.partial(exchange_kernel, seq, tensor, capacity, piece, parts, block, early_waves, norm),
        out_shape=(
            jax.ShapeDtypeStruct((slots - skipped, packed_width), BF16),
            jax.ShapeDtypeStruct(base_shape, F32),
            jax.ShapeDtypeStruct((8, slots), F32),
            jax.ShapeDtypeStruct((vocab_rows, resp), BF16),
            jax.ShapeDtypeStruct((resp, width), BF16),
            jax.ShapeDtypeStruct(hidden.shape, BF16),
            jax.ShapeDtypeStruct((1, 1), F32),
        ),
        in_specs=[vmem] * 9 + [hbm],
        out_specs=(hbm, hbm, vmem, vmem, vmem, vmem, vmem),
        scratch_shapes=[
            pltpu.VMEM((vocab_rows, width), BF16),
            pltpu.VMEM((slots, packed_width), BF16),
            pltpu.VMEM((seq * ROWS, half), BF16),
            pltpu.VMEM((vocab_rows, resp), F32),
            pltpu.VMEM((n, 8, resp), F32),
            pltpu.VMEM((n, 8, resp), F32),
            pltpu.VMEM((resp, width), F32),
            pltpu.VMEM((seq, resp // seq, width), F32),
            pltpu.VMEM((tensor, resp // seq, slab), F32),
            pltpu.VMEM((tensor, resp // seq, slab), F32),
            pltpu.VMEM((resp // seq, slab), F32),
            pltpu.VMEM((tensor, resp // seq, slab), F32),
            pltpu.SemaphoreType.DMA,
            pltpu.SemaphoreType.DMA,
            pltpu.SemaphoreType.DMA((TOKENS + WAVES,)),
            pltpu.SemaphoreType.DMA((TOKENS + WAVES,)),
        ]
        + (early_scratch if early_waves else []),
        compiler_params=pltpu.CompilerParams(
            collective_id=0, has_side_effects=True, vmem_limit_bytes=60 << 20
        ),
        name="exchange",
    )(
        targets.reshape(1, resp),
        branch.reshape(1, resp),
        pair_of_row.reshape(1, resp),
        ref_log_prob.reshape(1, resp),
        pair_weight.reshape(pairs, 1),
        token_ids.reshape(1, tokens),
        token_ids.reshape(tokens, 1),
        folded,
        token_grad,
        weight,
    )
    last = parts * subs - 1
    weight_grad = pl.pallas_call(
        functools.partial(weight_grad_kernel, parts, subs, skipped, norm),
        grid=(steps,),
        out_shape=jax.ShapeDtypeStruct(weight.shape, BF16),
        in_specs=[
            pl.BlockSpec((slots - skipped, block), lambda i: (0, jnp.minimum(i, last))),
            pl.BlockSpec((8, slots), lambda i: (0, 0)),
            pl.BlockSpec((vocab_rows, resp), lambda i: (0, 0)),
            pl.BlockSpec((resp, block), lambda i: (0, i)),
            pl.BlockSpec((1,) + base_shape[1:], lambda i: (jnp.minimum(i, base_shape[0] - 1), 0, 0)),
        ],
        out_specs=pl.BlockSpec((vocab_rows, block), lambda i: (0, i)),
        scratch_shapes=[
            pltpu.VMEM((vocab_rows, slots - skipped), BF16),
            pltpu.VMEM((subs, vocab_rows, block), F32),
        ],
        compiler_params=pltpu.CompilerParams(vmem_limit_bytes=56 << 20),
        name="weight_grad",
    )(arrived, tags, dlogits, gathered, base)
    return (loss.reshape(()), weight_grad, hidden_grad)


def solution(mesh):
    return jax.shard_map(
        shards,
        mesh=mesh,
        in_specs=(
            P(("seq", "tensor"), None),
            P("seq", None),
            P(),
            P(),
            P(),
            P(),
            P(),
            P(("seq", "tensor")),
            P(("seq", "tensor"), None),
        ),
        out_specs=(P(), P(("seq", "tensor"), None), P("seq", None)),
        check_vma=False,
    )
```

```python
import functools
import math

import jax
import jax.numpy as jnp
from jax import lax
from jax.experimental import pallas as pl
from jax.experimental.pallas import tpu as pltpu
from jax.sharding import PartitionSpec as P

dpo_beta = 0.1
LANES = 128
ROWS = 16
CHUNK = 128
TOKENS = 7
WAVES = 4
MESH = pl.DeviceIdType.MESH
F32, BF16 = jnp.float32, jnp.bfloat16


def pack_plan(capacity, tiles):
    for piece in range(tiles // 2, 0, -1):
        parts = tiles // piece - 1
        if tiles % piece == 0 and (ROWS - capacity) * parts >= capacity:
            return piece, parts
    raise ValueError("no packing")


def exchange_kernel(
    seq, tensor, capacity, piece, parts, block, early_waves, norm,
    targets, branch, pair_of_row, ref_log_prob, pair_weight, ids_row, ids_col, hidden, token_grad, weight_hbm,
    arrived, base_hbm, tags, dlogits, gathered, hidden_grad, loss,
    weight, packed, folded, logits, stat, stats, partial, seq_parts, sums, tensor_parts, done, pieces,
    load_sem, own_sem, send_sems, recv_sems, *early_scratch,
):
    n = seq * tensor
    vocab_rows, width = weight.shape
    resp = targets.shape[1]
    tokens = ids_row.shape[1]
    mine_seq, mine_tensor = lax.axis_index("seq"), lax.axis_index("tensor")
    me = mine_seq * tensor + mine_tensor

    core = lax.rem(mine_seq, 2)

    def exclusive_or(a, b, size):
        total = 0
        for bit in [1 << k for k in range(size.bit_length() - 1)]:
            total = total + lax.rem(lax.div(a, bit) + lax.div(b, bit), 2) * bit
        return total

    own_block = 1 - core

    def device(b):
        place = lax.rem(b, tensor)
        bits = lax.rem(place + 1 + core, 2) * (tensor // 2) + lax.div(place, 2)
        return (
            exclusive_or(mine_seq, lax.div(b, tensor), seq),
            exclusive_or(mine_tensor, bits, tensor),
        )

    def send(src, dst, kind, target):
        pltpu.make_async_remote_copy(
            src_ref=src, dst_ref=dst, send_sem=send_sems.at[kind], recv_sem=recv_sems.at[kind],
            device_id=target, device_id_type=MESH,
        ).start()

    def wait(sems, kind, ref):
        pltpu.make_async_copy(ref, ref, sems.at[kind]).wait()

    load = pltpu.make_async_copy(weight_hbm, weight, load_sem)
    load.start()
    barrier = pltpu.get_barrier_semaphore()

    def greet(rel, carry):
        peer = lax.rem(me + rel, n)
        pl.semaphore_signal(
            barrier, inc=1, device_id=(lax.div(peer, tensor), lax.rem(peer, tensor)), device_id_type=MESH
        )
        return carry

    lax.fori_loop(1, n, greet, 0)

    shift = vocab_rows.bit_length() - 1
    owner = jnp.right_shift(ids_row[...], shift)
    owner_col = jnp.right_shift(ids_col[...], shift)
    before = lax.broadcasted_iota(jnp.int32, (tokens, tokens), 0) < lax.broadcasted_iota(
        jnp.int32, (tokens, tokens), 1
    )
    slot = jnp.sum(jnp.where((owner_col == owner) & before, 1.0, 0.0), axis=0, keepdims=True).astype(jnp.int32)
    seq_bits = jnp.right_shift(owner, tensor.bit_length() - 1) ^ mine_seq
    tensor_bits = (owner & (tensor - 1)) ^ mine_tensor
    crosses = jnp.where(tensor_bits >= tensor // 2, 1, 0)
    rel_owner = seq_bits * tensor + (tensor_bits & (tensor // 2 - 1)) * 2 + ((crosses + 1 + core) & 1)
    spare = jnp.zeros_like(slot)
    for j in range(1, ROWS - capacity):
        spare = spare + jnp.where(slot >= j * parts, 1, 0)
    part_of = slot - spare * parts
    main_row = rel_owner * ROWS + slot
    spare_row = rel_owner * ROWS + capacity + spare
    label = (ids_row[...] - owner * vocab_rows + 1).astype(F32)
    piece_width = piece * LANES
    chunks = n * ROWS // CHUNK
    wave_rows = n * ROWS // WAVES
    if early_waves:
        early, base, rest, base_sems = early_scratch

    def exact_dot(left, right, dims):
        high = left.astype(BF16)
        low = (left - high.astype(F32)).astype(BF16)
        ones = right.astype(BF16)
        return lax.dot_general(high, ones, dims, preferred_element_type=F32) + lax.dot_general(
            low, ones, dims, preferred_element_type=F32
        )

    to_rel = lax.broadcasted_iota(jnp.int32, (n, tokens), 0) == rel_owner
    at_slot = jnp.where(lax.broadcasted_iota(jnp.int32, (resp, tokens), 0) == slot, 1.0, 0.0)
    stat[...] = jnp.zeros_like(stat)
    stat[:, 3, :] = exact_dot(jnp.where(to_rel, label, 0.0), at_slot, (((1,), (1,)), ((), ())))

    pl.semaphore_wait(barrier, n - 1)

    mine_rows = pl.ds(pl.multiple_of(mine_seq * ROWS, ROWS), ROWS)
    folded[mine_rows] = hidden[...]
    for k in range(1, seq):
        send(hidden, folded.at[mine_rows], 0, (lax.rem(mine_seq + k, seq), mine_tensor))

    def pack(wave, chunk, carry):
        first = pl.multiple_of(chunk * CHUNK, CHUNK)
        rows = first + lax.broadcasted_iota(jnp.int32, (CHUNK, tokens), 0)
        main = rows == main_row
        in_spare = rows == spare_row
        main_pick = jnp.where(main, 1.0, 0.0).astype(BF16)
        for part in range(parts):
            last = in_spare & (part_of == part)
            last_pick = jnp.where(last, 1.0, 0.0).astype(BF16)
            here = pl.ds(part * piece_width, piece_width)
            packed[pl.ds(first, CHUNK), here] = (
                jnp.dot(main_pick, token_grad[:, here], preferred_element_type=F32)
                + jnp.dot(
                    last_pick, token_grad[:, parts * piece_width :], preferred_element_type=F32
                )
            ).astype(BF16)

        return carry

    def pack_wave(wave):
        lax.fori_loop(wave * chunks // WAVES, (wave + 1) * chunks // WAVES, functools.partial(pack, wave), 0)

    def send_blocks(first_eighth, end_eighth):
        for eighth in range(first_eighth, end_eighth):
            wave = eighth * WAVES // 8

            def send_block(b, carry):
                src = pl.ds(pl.multiple_of(b * ROWS, ROWS), ROWS)
                if wave < early_waves:
                    land = early.at[src]
                else:
                    land = arrived.at[pl.ds(pl.multiple_of(b * ROWS - early_waves * wave_rows, ROWS), ROWS)]

                @pl.when(b != own_block)
                def _():
                    send(packed.at[src], land, TOKENS + wave, device(b))

                return carry

            lax.fori_loop(eighth * n // 8, (eighth + 1) * n // 8, send_block, 0)

    pack_wave(0)
    send_blocks(0, 1)
    own_rows = pl.ds(pl.multiple_of(own_block * ROWS, ROWS), ROWS)
    own = pltpu.make_async_copy(packed.at[own_rows], (early if early_waves else arrived).at[own_rows], own_sem)
    own.start()

    wait(recv_sems, 0, folded.at[pl.ds(0, (seq - 1) * ROWS)])
    half = width // 2
    for pair in range(seq // 2):
        both = folded[pair * 2 * ROWS : (pair + 1) * 2 * ROWS].astype(F32)
        rows = pl.ds(pair * ROWS, ROWS)
        gathered[rows, :half] = jnp.concatenate([both[0:8], both[16:24]], axis=0).astype(BF16)
        gathered[rows, half:] = jnp.concatenate([both[8:16], both[24:32]], axis=0).astype(BF16)
    load.wait()
    step = 6 * LANES
    logits[...] = jnp.zeros_like(logits)

    def add_logits(i, carry):
        columns = pl.ds(pl.multiple_of(i * step, step), step)
        logits[...] += lax.dot_general(
            weight[:, columns], gathered[:, columns], (((1,), (1,)), ((), ())), preferred_element_type=F32
        )
        return carry

    lax.fori_loop(0, width // step, add_logits, 0)
    value = logits[...]
    top = jnp.max(value, axis=0, keepdims=True)
    hit = lax.broadcasted_iota(jnp.int32, (vocab_rows, resp), 0) == targets[...] - me * vocab_rows
    stat[:, 0, :] = jnp.broadcast_to(top, (n, resp))
    stat[:, 1, :] = jnp.broadcast_to(jnp.sum(jnp.exp(value - top), axis=0, keepdims=True), (n, resp))
    stat[:, 2, :] = jnp.broadcast_to(jnp.sum(jnp.where(hit, value, 0.0), axis=0, keepdims=True), (n, resp))
    stats[pl.ds(me, 1)] = stat[pl.ds(own_block, 1)]

    def send_stat(rel, carry):
        @pl.when(rel != own_block)
        def _():
            send(stat.at[rel], stats.at[me], 3, device(rel))

        return carry

    lax.fori_loop(0, n, send_stat, 0)
    send_blocks(1, 2)
    pack_wave(1)
    wait(recv_sems, 3, stats.at[pl.ds(0, n - 1)])
    tops = stats[:, 0, :]
    row_top = jnp.max(tops, axis=0, keepdims=True)
    row_total = jnp.sum(jnp.exp(tops - row_top) * stats[:, 1, :], axis=0, keepdims=True)
    target_logit = jnp.sum(stats[:, 2, :], axis=0, keepdims=True)
    log_prob = target_logit - row_top - jnp.log(row_total)
    sign = jnp.where(branch[...] == 1, 1.0, 0.0) - jnp.where(branch[...] == 2, 1.0, 0.0)
    pairs = pair_weight.shape[0]
    member = lax.broadcasted_iota(jnp.int32, (pairs, resp), 0) == pair_of_row[...]
    margin = jnp.sum(jnp.where(member, sign * (log_prob - ref_log_prob[...]), 0.0), axis=1, keepdims=True)
    z = -dpo_beta * margin
    softplus = jnp.maximum(z, 0.0) + jnp.log1p(jnp.exp(-jnp.abs(z)))
    loss[...] = jnp.sum(pair_weight[...] * softplus, axis=0, keepdims=True)
    push_back = pair_weight[...] * lax.logistic(z)
    row_scale = -dpo_beta * sign * jnp.sum(jnp.where(member, push_back, 0.0), axis=0, keepdims=True)
    probs = jnp.exp(value - row_top) / row_total
    rounded = (row_scale * (jnp.where(hit, 1.0, 0.0) - probs)).astype(BF16)
    dlogits[...] = rounded
    by_row = jnp.transpose(rounded.astype(F32)).astype(BF16)

    def add_partial(i, carry):
        columns = pl.ds(pl.multiple_of(i * step, step), step)
        partial[:, columns] = jnp.dot(by_row, weight[:, columns], preferred_element_type=F32)
        return carry

    lax.fori_loop(0, width // step, add_partial, 0)
    share = resp // seq
    for k in range(1, seq):
        peer = lax.rem(mine_seq + k, seq)
        rows = pl.ds(pl.multiple_of(peer * share, share), share)
        send(partial.at[rows], seq_parts.at[mine_seq], 4, (peer, mine_tensor))
    send_blocks(2, 4)
    pack_wave(2)
    rows = pl.ds(pl.multiple_of(mine_seq * share, share), share)
    seq_parts[pl.ds(mine_seq, 1)] = partial[rows, :][None]
    wait(recv_sems, 4, seq_parts.at[pl.ds(0, seq - 1)])
    total = seq_parts[0]
    for k in range(1, seq):
        total = total + seq_parts[k]
    slab = sums.shape[2]
    cuts = [(i, i * slab, min((i + 1) * slab, width)) for i in range(tensor) if i * slab < width]
    sums[...] = jnp.zeros_like(sums)
    for i, low, high in cuts:
        sums[i, :, : high - low] = total[:, low:high]
    for k in range(1, tensor):
        peer = lax.rem(mine_tensor + k, tensor)
        send(sums.at[peer], tensor_parts.at[mine_tensor], 5, (mine_seq, peer))
    send_blocks(4, 5)
    pack_wave(3)
    tensor_parts[pl.ds(mine_tensor, 1)] = sums[pl.ds(mine_tensor, 1)]
    wait(recv_sems, 5, tensor_parts.at[pl.ds(0, tensor - 1)])
    total = tensor_parts[0]
    for k in range(1, tensor):
        total = total + tensor_parts[k]
    done[...] = total
    pieces[pl.ds(mine_tensor, 1)] = total[None]
    for k in range(1, tensor):
        send(done, pieces.at[mine_tensor], 6, (mine_seq, lax.rem(mine_tensor + k, tensor)))
    send_blocks(5, 8)

    slots = n * ROWS
    column = lax.broadcasted_iota(jnp.int32, (resp, slots), 1)
    column = column - jnp.right_shift(column, ROWS.bit_length() - 1) * ROWS
    wanted = lax.broadcasted_iota(jnp.int32, (resp, slots), 0)
    came = lax.broadcasted_iota(jnp.int32, (n, slots), 1)
    came = jnp.right_shift(came, ROWS.bit_length() - 1)
    place = came & (tensor - 1)
    seq_bits = jnp.right_shift(came, tensor.bit_length() - 1)
    crosses = (place + 1 + ((seq_bits + core) & 1)) & 1
    tensor_bits = crosses * (tensor // 2) + jnp.right_shift(place, 1)
    came = (seq_bits ^ mine_seq) * tensor + (tensor_bits ^ mine_tensor)
    came = came == lax.broadcasted_iota(jnp.int32, (n, slots), 0)
    sent_labels = stats[:, 3, :]
    tags[...] = jnp.zeros_like(tags)
    for k in range(parts + 1):
        if k == 0:
            chosen = (column == wanted) & (column < capacity)
        else:
            chosen = (column >= capacity) & (wanted == (column - capacity) * parts + (k - 1))
        spread = exact_dot(sent_labels, jnp.where(chosen, 1.0, 0.0), (((1,), (0,)), ((), ())))
        tags[k : k + 1, :] = jnp.sum(jnp.where(came, spread, 0.0), axis=0, keepdims=True)

    own.wait()

    def wait_wave(wave):
        low, high = wave * wave_rows + (ROWS if wave == 0 else 0), (wave + 1) * wave_rows
        wait(send_sems, TOKENS + wave, packed.at[pl.ds(low, high - low)])
        if wave < early_waves:
            wait(recv_sems, TOKENS + wave, early.at[pl.ds(low, high - low)])
        else:
            wait(recv_sems, TOKENS + wave, arrived.at[pl.ds(low - early_waves * wave_rows, high - low)])

    if early_waves:
        for wave in range(early_waves):
            wait_wave(wave)
        count = early_waves * wave_rows
        vocab = lax.broadcasted_iota(jnp.int32, (vocab_rows, count), 0).astype(F32) + 1.0
        main_pick = jnp.where(vocab == tags[0:1, :count], 1.0, 0.0).astype(BF16)
        subs = piece_width // block
        rest[...] = jnp.zeros_like(rest)
        stores = []
        for i in range((parts + 1) * subs):
            here = pl.ds(i * block, block)
            head = jnp.dot(dlogits[...], gathered[:, here], preferred_element_type=F32)
            if i < parts * subs:
                part = i // subs
                last_pick = jnp.where(vocab == tags[part + 1 : part + 2, :count], 1.0, 0.0).astype(BF16)
                base[i] = head + norm * jnp.dot(main_pick, early[:, here], preferred_element_type=F32)
                rest[i % subs] += jnp.dot(last_pick, early[:, here], preferred_element_type=F32)
            else:
                base[i] = head + norm * rest[i % subs]
            stores.append(pltpu.make_async_copy(base.at[i], base_hbm.at[i], base_sems.at[i]))
            stores[-1].start()
        for store in stores:
            store.wait()
    wait(recv_sems, 6, pieces.at[pl.ds(0, tensor - 1)])
    for i, low, high in cuts:
        hidden_grad[:, low:high] = pieces[i, :, : high - low].astype(BF16)

    for wave in range(early_waves, WAVES):
        wait_wave(wave)
    wait(send_sems, 0, folded.at[pl.ds(0, (seq - 1) * ROWS)])
    wait(send_sems, 3, stats.at[pl.ds(0, n - 1)])
    wait(send_sems, 4, seq_parts.at[pl.ds(0, seq - 1)])
    wait(send_sems, 5, tensor_parts.at[pl.ds(0, tensor - 1)])
    wait(send_sems, 6, pieces.at[pl.ds(0, tensor - 1)])


def weight_grad_kernel(parts, subs, skipped, norm, arrived, tags, dlogits, gathered, base, out, main_pick, rest):
    i = pl.program_id(0)
    vocab_rows, slots = main_pick.shape
    vocab = lax.broadcasted_iota(jnp.int32, (vocab_rows, slots), 0).astype(F32) + 1.0

    @pl.when(i == 0)
    def _():
        main_pick[...] = jnp.where(vocab == tags[0:1, skipped:], 1.0, 0.0).astype(BF16)
        rest[...] = jnp.zeros_like(rest)

    if skipped:
        before = base[0]
    else:
        before = jnp.dot(dlogits[...], gathered[...], preferred_element_type=F32)
    sub = lax.rem(i, subs)

    @pl.when(i < parts * subs)
    def _():
        block = arrived[...]
        out[...] = (before + norm * jnp.dot(main_pick[...], block, preferred_element_type=F32)).astype(BF16)
        part = lax.div(i, subs)
        last_pick = jnp.where(vocab == tags[pl.ds(part + 1, 1), :][:, skipped:], 1.0, 0.0).astype(BF16)
        rest[pl.ds(sub, 1)] += jnp.dot(last_pick, block, preferred_element_type=F32)[None]

    @pl.when(i >= parts * subs)
    def _():
        out[...] = (before + norm * rest[pl.ds(sub, 1)][0]).astype(BF16)


def shards(
    weight, hidden, targets, branch, pair_of_row, ref_log_prob, pair_weight, token_ids, token_grad
):
    vocab_rows, width = weight.shape
    seq, tensor = lax.axis_size("seq"), lax.axis_size("tensor")
    n = seq * tensor
    resp, tokens, pairs = targets.shape[0], token_ids.shape[0], pair_weight.shape[0]
    capacity = max(2, (2 * tokens + n - 1) // n)
    tiles = width // LANES
    piece, parts = pack_plan(capacity, tiles)
    subs = next(k for k in range(1, piece + 1) if piece % k == 0 and piece // k <= 8)
    block = piece // subs * LANES
    packed_width = parts * piece * LANES
    slab = (tiles + tensor - 1) // tensor * LANES
    half = width // 2
    folded = jnp.concatenate([hidden[:, :half], hidden[:, half:]], axis=0)
    vmem, hbm = pl.BlockSpec(memory_space=pltpu.VMEM), pl.BlockSpec(memory_space=pl.ANY)
    norm = math.sqrt(width)
    slots = n * ROWS
    early_waves = WAVES - 1 if slots * packed_width * 2 <= 8 << 20 else 0
    skipped = early_waves * slots // WAVES
    steps = (parts + 1) * subs
    base_shape = (steps, vocab_rows, block) if early_waves else (1, 8, LANES)
    early_scratch = [
        pltpu.VMEM((skipped, packed_width), BF16),
        pltpu.VMEM(base_shape, F32),
        pltpu.VMEM((subs, vocab_rows, block), F32),
        pltpu.SemaphoreType.DMA((steps,)),
    ]
    arrived, base, tags, dlogits, gathered, hidden_grad, loss = pl.pallas_call(
        functools.partial(exchange_kernel, seq, tensor, capacity, piece, parts, block, early_waves, norm),
        out_shape=(
            jax.ShapeDtypeStruct((slots - skipped, packed_width), BF16),
            jax.ShapeDtypeStruct(base_shape, F32),
            jax.ShapeDtypeStruct((8, slots), F32),
            jax.ShapeDtypeStruct((vocab_rows, resp), BF16),
            jax.ShapeDtypeStruct((resp, width), BF16),
            jax.ShapeDtypeStruct(hidden.shape, BF16),
            jax.ShapeDtypeStruct((1, 1), F32),
        ),
        in_specs=[vmem] * 9 + [hbm],
        out_specs=(hbm, hbm, vmem, vmem, vmem, vmem, vmem),
        scratch_shapes=[
            pltpu.VMEM((vocab_rows, width), BF16),
            pltpu.VMEM((slots, packed_width), BF16),
            pltpu.VMEM((seq * ROWS, half), BF16),
            pltpu.VMEM((vocab_rows, resp), F32),
            pltpu.VMEM((n, 8, resp), F32),
            pltpu.VMEM((n, 8, resp), F32),
            pltpu.VMEM((resp, width), F32),
            pltpu.VMEM((seq, resp // seq, width), F32),
            pltpu.VMEM((tensor, resp // seq, slab), F32),
            pltpu.VMEM((tensor, resp // seq, slab), F32),
            pltpu.VMEM((resp // seq, slab), F32),
            pltpu.VMEM((tensor, resp // seq, slab), F32),
            pltpu.SemaphoreType.DMA,
            pltpu.SemaphoreType.DMA,
            pltpu.SemaphoreType.DMA((TOKENS + WAVES,)),
            pltpu.SemaphoreType.DMA((TOKENS + WAVES,)),
        ]
        + (early_scratch if early_waves else []),
        compiler_params=pltpu.CompilerParams(
            collective_id=0, has_side_effects=True, vmem_limit_bytes=60 << 20
        ),
        name="exchange",
    )(
        targets.reshape(1, resp),
        branch.reshape(1, resp),
        pair_of_row.reshape(1, resp),
        ref_log_prob.reshape(1, resp),
        pair_weight.reshape(pairs, 1),
        token_ids.reshape(1, tokens),
        token_ids.reshape(tokens, 1),
        folded,
        token_grad,
        weight,
    )
    last = parts * subs - 1
    weight_grad = pl.pallas_call(
        functools.partial(weight_grad_kernel, parts, subs, skipped, norm),
        grid=(steps,),
        out_shape=jax.ShapeDtypeStruct(weight.shape, BF16),
        in_specs=[
            pl.BlockSpec((slots - skipped, block), lambda i: (0, jnp.minimum(i, last))),
            pl.BlockSpec((8, slots), lambda i: (0, 0)),
            pl.BlockSpec((vocab_rows, resp), lambda i: (0, 0)),
            pl.BlockSpec((resp, block), lambda i: (0, i)),
            pl.BlockSpec((1,) + base_shape[1:], lambda i: (jnp.minimum(i, base_shape[0] - 1), 0, 0)),
        ],
        out_specs=pl.BlockSpec((vocab_rows, block), lambda i: (0, i)),
        scratch_shapes=[
            pltpu.VMEM((vocab_rows, slots - skipped), BF16),
            pltpu.VMEM((subs, vocab_rows, block), F32),
        ],
        compiler_params=pltpu.CompilerParams(vmem_limit_bytes=56 << 20),
        name="weight_grad",
    )(arrived, tags, dlogits, gathered, base)
    return (loss.reshape(()), weight_grad, hidden_grad)


def solution(mesh):
    return jax.shard_map(
        shards,
        mesh=mesh,
        in_specs=(
            P(("seq", "tensor"), None),
            P("seq", None),
            P(),
            P(),
            P(),
            P(),
            P(),
            P(("seq", "tensor")),
            P(("seq", "tensor"), None),
        ),
        out_specs=(P(), P(("seq", "tensor"), None), P("seq", None)),
        check_vma=False,
    )
```

```python
import functools
import math

import jax
import jax.numpy as jnp
from jax import lax
from jax.experimental import pallas as pl
from jax.experimental.pallas import tpu as pltpu
from jax.sharding import PartitionSpec as P

dpo_beta = 0.1
LANES = 128
ROWS = 16
CHUNK = 128
TOKENS = 7
WAVES = 4
MESH = pl.DeviceIdType.MESH
F32, BF16 = jnp.float32, jnp.bfloat16


def pack_plan(capacity, tiles):
    for piece in range(tiles // 2, 0, -1):
        parts = tiles // piece - 1
        if tiles % piece == 0 and (ROWS - capacity) * parts >= capacity:
            return piece, parts
    raise ValueError("no packing")


def unpack_pick(capacity, parts, part):
    to = lax.broadcasted_iota(jnp.int32, (CHUNK, CHUNK), 0)
    source = lax.broadcasted_iota(jnp.int32, (CHUNK, CHUNK), 1)
    bits = ROWS.bit_length() - 1
    spare = (source & (ROWS - 1)) - capacity
    chosen = (
        (jnp.right_shift(to, bits) == jnp.right_shift(source, bits))
        & (spare >= 0)
        & ((to & (ROWS - 1)) == spare * parts + part)
    )
    return jnp.where(chosen, 1.0, 0.0).astype(BF16)


def exchange_kernel(
    seq, tensor, capacity, piece, parts, block, early_waves, norm,
    targets, branch, pair_of_row, ref_log_prob, pair_weight_row, ids_row, hidden_rows, token_grad, weight_hbm,
    arrived, base_hbm, tags, dlogits, gathered, hidden_grad, loss,
    weight, packed, hidden, folded, logits, stat, stats, partial, seq_parts, sums, tensor_parts, done, pieces,
    load_sem, own_sem, send_sems, recv_sems, *early_scratch,
):
    n = seq * tensor
    vocab_rows, width = weight.shape
    resp = targets.shape[1]
    tokens = ids_row.shape[1]
    mine_seq, mine_tensor = lax.axis_index("seq"), lax.axis_index("tensor")
    me = mine_seq * tensor + mine_tensor

    core = lax.rem(mine_seq, 2)

    def exclusive_or(a, b, size):
        total = 0
        for bit in [1 << k for k in range(size.bit_length() - 1)]:
            total = total + lax.rem(lax.div(a, bit) + lax.div(b, bit), 2) * bit
        return total

    own_block = 1 - core

    def device(b):
        place = lax.rem(b, tensor)
        bits = lax.rem(place + 1 + core, 2) * (tensor // 2) + lax.div(place, 2)
        return (
            exclusive_or(mine_seq, lax.div(b, tensor), seq),
            exclusive_or(mine_tensor, bits, tensor),
        )

    def send(src, dst, kind, target):
        pltpu.make_async_remote_copy(
            src_ref=src, dst_ref=dst, send_sem=send_sems.at[kind], recv_sem=recv_sems.at[kind],
            device_id=target, device_id_type=MESH,
        ).start()

    def wait(sems, kind, ref):
        pltpu.make_async_copy(ref, ref, sems.at[kind]).wait()

    load = pltpu.make_async_copy(weight_hbm, weight, load_sem)
    load.start()
    half = width // 2
    whole = hidden_rows[...].astype(F32)
    hidden[...] = jnp.concatenate([whole[:, :half], whole[:, half:]], axis=0).astype(BF16)
    folded[pl.ds(pl.multiple_of(mine_seq * ROWS, ROWS), ROWS)] = hidden[...]
    barrier = pltpu.get_barrier_semaphore()

    def greet(rel, carry):
        peer = lax.rem(me + rel, n)
        pl.semaphore_signal(
            barrier, inc=1, device_id=(lax.div(peer, tensor), lax.rem(peer, tensor)), device_id_type=MESH
        )
        return carry

    lax.fori_loop(1, n, greet, 0)

    shift = vocab_rows.bit_length() - 1
    owner = jnp.right_shift(ids_row[...], shift)
    before = lax.broadcasted_iota(jnp.int32, (tokens, tokens), 0) < lax.broadcasted_iota(
        jnp.int32, (tokens, tokens), 1
    )
    to_owner = lax.broadcasted_iota(jnp.int32, (n, tokens), 0) == owner
    earlier = jnp.dot(
        jnp.where(to_owner, 1.0, 0.0).astype(BF16),
        jnp.where(before, 1.0, 0.0).astype(BF16),
        preferred_element_type=F32,
    )
    slot = jnp.sum(jnp.where(to_owner, earlier, 0.0), axis=0, keepdims=True).astype(jnp.int32)
    seq_bits = jnp.right_shift(owner, tensor.bit_length() - 1) ^ mine_seq
    tensor_bits = (owner & (tensor - 1)) ^ mine_tensor
    crosses = jnp.where(tensor_bits >= tensor // 2, 1, 0)
    rel_owner = seq_bits * tensor + (tensor_bits & (tensor // 2 - 1)) * 2 + ((crosses + 1 + core) & 1)
    spare = jnp.zeros_like(slot)
    for j in range(1, ROWS - capacity):
        spare = spare + jnp.where(slot >= j * parts, 1, 0)
    part_of = slot - spare * parts
    main_row = rel_owner * ROWS + slot
    spare_row = rel_owner * ROWS + capacity + spare
    label = (ids_row[...] - owner * vocab_rows + 1).astype(F32)
    piece_width = piece * LANES
    chunks = n * ROWS // CHUNK
    wave_rows = n * ROWS // WAVES
    if early_waves:
        early, base, rest, base_sems = early_scratch

    def exact_dot(left, right, dims):
        high = left.astype(BF16)
        low = (left - high.astype(F32)).astype(BF16)
        ones = right.astype(BF16)
        return lax.dot_general(high, ones, dims, preferred_element_type=F32) + lax.dot_general(
            low, ones, dims, preferred_element_type=F32
        )

    to_rel = lax.broadcasted_iota(jnp.int32, (n, tokens), 0) == rel_owner
    at_slot = jnp.where(lax.broadcasted_iota(jnp.int32, (resp, tokens), 0) == slot, 1.0, 0.0)
    stat[...] = jnp.zeros_like(stat)
    stat[:, 3, :] = exact_dot(jnp.where(to_rel, label, 0.0), at_slot, (((1,), (1,)), ((), ())))

    pl.semaphore_wait(barrier, n - 1)

    mine_rows = pl.ds(pl.multiple_of(mine_seq * ROWS, ROWS), ROWS)
    for k in range(1, seq):
        send(hidden, folded.at[mine_rows], 0, (lax.rem(mine_seq + k, seq), mine_tensor))

    def pack(wave, chunk, carry):
        first = pl.multiple_of(chunk * CHUNK, CHUNK)
        rows = first + lax.broadcasted_iota(jnp.int32, (CHUNK, tokens), 0)
        main = rows == main_row
        in_spare = rows == spare_row
        main_pick = jnp.where(main, 1.0, 0.0).astype(BF16)
        for part in range(parts):
            last = in_spare & (part_of == part)
            last_pick = jnp.where(last, 1.0, 0.0).astype(BF16)
            here = pl.ds(part * piece_width, piece_width)
            packed[pl.ds(first, CHUNK), here] = (
                jnp.dot(main_pick, token_grad[:, here], preferred_element_type=F32)
                + jnp.dot(
                    last_pick, token_grad[:, parts * piece_width :], preferred_element_type=F32
                )
            ).astype(BF16)

        return carry

    def pack_wave(wave):
        lax.fori_loop(wave * chunks // WAVES, (wave + 1) * chunks // WAVES, functools.partial(pack, wave), 0)

    def send_blocks(first_eighth, end_eighth):
        for eighth in range(first_eighth, end_eighth):
            wave = eighth * WAVES // 8

            def send_block(b, carry):
                src = pl.ds(pl.multiple_of(b * ROWS, ROWS), ROWS)
                if wave < early_waves:
                    land = early.at[src]
                else:
                    land = arrived.at[pl.ds(pl.multiple_of(b * ROWS - early_waves * wave_rows, ROWS), ROWS)]

                @pl.when(b != own_block)
                def _():
                    send(packed.at[src], land, TOKENS + wave, device(b))

                return carry

            lax.fori_loop(eighth * n // 8, (eighth + 1) * n // 8, send_block, 0)

    pack_wave(0)
    send_blocks(0, 1)
    own_rows = pl.ds(pl.multiple_of(own_block * ROWS, ROWS), ROWS)
    own = pltpu.make_async_copy(packed.at[own_rows], (early if early_waves else arrived).at[own_rows], own_sem)
    own.start()

    wait(recv_sems, 0, folded.at[pl.ds(0, (seq - 1) * ROWS)])
    for pair in range(seq // 2):
        both = folded[pair * 2 * ROWS : (pair + 1) * 2 * ROWS].astype(F32)
        rows = pl.ds(pair * ROWS, ROWS)
        gathered[rows, :half] = jnp.concatenate([both[0:8], both[16:24]], axis=0).astype(BF16)
        gathered[rows, half:] = jnp.concatenate([both[8:16], both[24:32]], axis=0).astype(BF16)
    load.wait()
    step = 6 * LANES
    logits[...] = jnp.zeros_like(logits)

    def add_logits(i, carry):
        columns = pl.ds(pl.multiple_of(i * step, step), step)
        logits[...] += lax.dot_general(
            weight[:, columns], gathered[:, columns], (((1,), (1,)), ((), ())), preferred_element_type=F32
        )
        return carry

    lax.fori_loop(0, width // step, add_logits, 0)
    value = logits[...]
    top = jnp.max(value, axis=0, keepdims=True)
    hit = lax.broadcasted_iota(jnp.int32, (vocab_rows, resp), 0) == targets[...] - me * vocab_rows
    stat[:, 0, :] = jnp.broadcast_to(top, (n, resp))
    stat[:, 1, :] = jnp.broadcast_to(jnp.sum(jnp.exp(value - top), axis=0, keepdims=True), (n, resp))
    stat[:, 2, :] = jnp.broadcast_to(jnp.sum(jnp.where(hit, value, 0.0), axis=0, keepdims=True), (n, resp))
    stats[pl.ds(me, 1)] = stat[pl.ds(own_block, 1)]

    def send_stat(rel, carry):
        @pl.when(rel != own_block)
        def _():
            send(stat.at[rel], stats.at[me], 3, device(rel))

        return carry

    lax.fori_loop(0, n, send_stat, 0)
    send_blocks(1, 2)
    pack_wave(1)
    wait(recv_sems, 3, stats.at[pl.ds(0, n - 1)])
    tops = stats[:, 0, :]
    row_top = jnp.max(tops, axis=0, keepdims=True)
    row_total = jnp.sum(jnp.exp(tops - row_top) * stats[:, 1, :], axis=0, keepdims=True)
    target_logit = jnp.sum(stats[:, 2, :], axis=0, keepdims=True)
    log_prob = target_logit - row_top - jnp.log(row_total)
    sign = jnp.where(branch[...] == 1, 1.0, 0.0) - jnp.where(branch[...] == 2, 1.0, 0.0)
    pairs = pair_weight_row.shape[1]
    same = lax.broadcasted_iota(jnp.int32, (pairs, pairs), 0) == lax.broadcasted_iota(
        jnp.int32, (pairs, pairs), 1
    )
    pair_weight = jnp.sum(jnp.where(same, pair_weight_row[...], 0.0), axis=1, keepdims=True)
    member = lax.broadcasted_iota(jnp.int32, (pairs, resp), 0) == pair_of_row[...]
    margin = jnp.sum(jnp.where(member, sign * (log_prob - ref_log_prob[...]), 0.0), axis=1, keepdims=True)
    z = -dpo_beta * margin
    softplus = jnp.maximum(z, 0.0) + jnp.log1p(jnp.exp(-jnp.abs(z)))
    loss[...] = jnp.sum(pair_weight * softplus, axis=0, keepdims=True)
    push_back = pair_weight * lax.logistic(z)
    row_scale = -dpo_beta * sign * jnp.sum(jnp.where(member, push_back, 0.0), axis=0, keepdims=True)
    probs = jnp.exp(value - row_top) / row_total
    rounded = (row_scale * (jnp.where(hit, 1.0, 0.0) - probs)).astype(BF16)
    dlogits[...] = rounded
    by_row = jnp.transpose(rounded.astype(F32)).astype(BF16)

    def add_partial(i, carry):
        columns = pl.ds(pl.multiple_of(i * step, step), step)
        partial[:, columns] = jnp.dot(by_row, weight[:, columns], preferred_element_type=F32)
        return carry

    lax.fori_loop(0, width // step, add_partial, 0)
    share = resp // seq
    for k in range(1, seq):
        peer = lax.rem(mine_seq + k, seq)
        rows = pl.ds(pl.multiple_of(peer * share, share), share)
        send(partial.at[rows], seq_parts.at[mine_seq], 4, (peer, mine_tensor))
    send_blocks(2, 4)
    pack_wave(2)
    rows = pl.ds(pl.multiple_of(mine_seq * share, share), share)
    seq_parts[pl.ds(mine_seq, 1)] = partial[rows, :][None]
    wait(recv_sems, 4, seq_parts.at[pl.ds(0, seq - 1)])
    total = seq_parts[0]
    for k in range(1, seq):
        total = total + seq_parts[k]
    slab = sums.shape[2]
    cuts = [(i, i * slab, min((i + 1) * slab, width)) for i in range(tensor) if i * slab < width]
    sums[...] = jnp.zeros_like(sums)
    for i, low, high in cuts:
        sums[i, :, : high - low] = total[:, low:high]
    for k in range(1, tensor):
        peer = lax.rem(mine_tensor + k, tensor)
        send(sums.at[peer], tensor_parts.at[mine_tensor], 5, (mine_seq, peer))
    send_blocks(4, 5)
    pack_wave(3)
    tensor_parts[pl.ds(mine_tensor, 1)] = sums[pl.ds(mine_tensor, 1)]
    wait(recv_sems, 5, tensor_parts.at[pl.ds(0, tensor - 1)])
    total = tensor_parts[0]
    for k in range(1, tensor):
        total = total + tensor_parts[k]
    done[...] = total
    pieces[pl.ds(mine_tensor, 1)] = total[None]
    for k in range(1, tensor):
        send(done, pieces.at[mine_tensor], 6, (mine_seq, lax.rem(mine_tensor + k, tensor)))
    send_blocks(5, 8)

    slots = n * ROWS
    column = lax.broadcasted_iota(jnp.int32, (resp, slots), 1)
    column = column - jnp.right_shift(column, ROWS.bit_length() - 1) * ROWS
    wanted = lax.broadcasted_iota(jnp.int32, (resp, slots), 0)
    came = lax.broadcasted_iota(jnp.int32, (n, slots), 1)
    came = jnp.right_shift(came, ROWS.bit_length() - 1)
    place = came & (tensor - 1)
    seq_bits = jnp.right_shift(came, tensor.bit_length() - 1)
    crosses = (place + 1 + ((seq_bits + core) & 1)) & 1
    tensor_bits = crosses * (tensor // 2) + jnp.right_shift(place, 1)
    came = (seq_bits ^ mine_seq) * tensor + (tensor_bits ^ mine_tensor)
    came = came == lax.broadcasted_iota(jnp.int32, (n, slots), 0)
    sent_labels = stats[:, 3, :]
    tags[...] = jnp.zeros_like(tags)
    chosen = (column == wanted) & (column < capacity)
    spread = exact_dot(sent_labels, jnp.where(chosen, 1.0, 0.0), (((1,), (0,)), ((), ())))
    tags[0:1, :] = jnp.sum(jnp.where(came, spread, 0.0), axis=0, keepdims=True)

    own.wait()

    def wait_wave(wave):
        low, high = wave * wave_rows + (ROWS if wave == 0 else 0), (wave + 1) * wave_rows
        wait(send_sems, TOKENS + wave, packed.at[pl.ds(low, high - low)])
        if wave < early_waves:
            wait(recv_sems, TOKENS + wave, early.at[pl.ds(low, high - low)])
        else:
            wait(recv_sems, TOKENS + wave, arrived.at[pl.ds(low - early_waves * wave_rows, high - low)])

    if early_waves:
        for wave in range(early_waves):
            wait_wave(wave)
        count = early_waves * wave_rows
        vocab = lax.broadcasted_iota(jnp.int32, (vocab_rows, count), 0).astype(F32) + 1.0
        main_pick = jnp.where(vocab == tags[0:1, :count], 1.0, 0.0).astype(BF16)
        subs = piece_width // block
        picks = [unpack_pick(capacity, parts, part) for part in range(parts)]
        for sub in range(subs):
            for low in range(0, count, CHUNK):
                last = jnp.zeros((CHUNK, block), F32)
                for part in range(parts):
                    here = pl.ds((part * subs + sub) * block, block)
                    last = last + jnp.dot(picks[part], early[low : low + CHUNK, here], preferred_element_type=F32)
                rest[sub, low : low + CHUNK, :] = last.astype(BF16)
        stores = []
        for i in range((parts + 1) * subs):
            here = pl.ds(i * block, block)
            rows = early[:, here] if i < parts * subs else rest[i % subs]
            head = jnp.dot(dlogits[...], gathered[:, here], preferred_element_type=F32)
            base[i] = head + norm * jnp.dot(main_pick, rows, preferred_element_type=F32)
            stores.append(pltpu.make_async_copy(base.at[i], base_hbm.at[i], base_sems.at[i]))
            stores[-1].start()
        for store in stores:
            store.wait()
    wait(recv_sems, 6, pieces.at[pl.ds(0, tensor - 1)])
    for i, low, high in cuts:
        hidden_grad[:, low:high] = pieces[i, :, : high - low].astype(BF16)

    for wave in range(early_waves, WAVES):
        wait_wave(wave)
    wait(send_sems, 0, folded.at[pl.ds(0, (seq - 1) * ROWS)])
    wait(send_sems, 3, stats.at[pl.ds(0, n - 1)])
    wait(send_sems, 4, seq_parts.at[pl.ds(0, seq - 1)])
    wait(send_sems, 5, tensor_parts.at[pl.ds(0, tensor - 1)])
    wait(send_sems, 6, pieces.at[pl.ds(0, tensor - 1)])


def weight_grad_kernel(capacity, parts, subs, skipped, norm, arrived, tags, dlogits, gathered, base, out, main_pick, rest):
    i = pl.program_id(0)
    vocab_rows, slots = main_pick.shape
    vocab = lax.broadcasted_iota(jnp.int32, (vocab_rows, slots), 0).astype(F32) + 1.0

    @pl.when(i == 0)
    def _():
        main_pick[...] = jnp.where(vocab == tags[0:1, skipped:], 1.0, 0.0).astype(BF16)
        rest[...] = jnp.zeros_like(rest)

    if skipped:
        before = base[0]
    else:
        before = jnp.dot(dlogits[...], gathered[...], preferred_element_type=F32)
    sub = lax.rem(i, subs)

    def store(rows):
        out[...] = (before + norm * jnp.dot(main_pick[...], rows, preferred_element_type=F32)).astype(BF16)

    @pl.when(i < parts * subs)
    def _():
        store(arrived[...])
        pick = unpack_pick(capacity, parts, lax.div(i, subs))

        def unpack(chunk, carry):
            rows = pl.ds(pl.multiple_of(chunk * CHUNK, CHUNK), CHUNK)
            moved = jnp.dot(pick, arrived[rows, :], preferred_element_type=F32)
            rest[sub, rows, :] = (rest[sub, rows, :].astype(F32) + moved).astype(BF16)
            return carry

        lax.fori_loop(0, slots // CHUNK, unpack, 0)

    @pl.when(i >= parts * subs)
    def _():
        store(rest[sub])


def shards(
    weight, hidden, targets, branch, pair_of_row, ref_log_prob, pair_weight, token_ids, token_grad
):
    vocab_rows, width = weight.shape
    seq, tensor = lax.axis_size("seq"), lax.axis_size("tensor")
    n = seq * tensor
    resp, tokens, pairs = targets.shape[0], token_ids.shape[0], pair_weight.shape[0]
    capacity = max(2, (2 * tokens + n - 1) // n)
    tiles = width // LANES
    piece, parts = pack_plan(capacity, tiles)
    subs = next(k for k in range(1, piece + 1) if piece % k == 0 and piece // k <= 8)
    block = piece // subs * LANES
    packed_width = parts * piece * LANES
    slab = (tiles + tensor - 1) // tensor * LANES
    half = width // 2
    vmem, hbm = pl.BlockSpec(memory_space=pltpu.VMEM), pl.BlockSpec(memory_space=pl.ANY)
    norm = math.sqrt(width)
    slots = n * ROWS
    early_waves = WAVES - 1 if slots * packed_width * 2 <= 8 << 20 else 0
    skipped = early_waves * slots // WAVES
    steps = (parts + 1) * subs
    base_shape = (steps, vocab_rows, block) if early_waves else (1, 8, LANES)
    early_scratch = [
        pltpu.VMEM((skipped, packed_width), BF16),
        pltpu.VMEM(base_shape, F32),
        pltpu.VMEM((subs, skipped, block), BF16),
        pltpu.SemaphoreType.DMA((steps,)),
    ]
    arrived, base, tags, dlogits, gathered, hidden_grad, loss = pl.pallas_call(
        functools.partial(exchange_kernel, seq, tensor, capacity, piece, parts, block, early_waves, norm),
        out_shape=(
            jax.ShapeDtypeStruct((slots - skipped, packed_width), BF16),
            jax.ShapeDtypeStruct(base_shape, F32),
            jax.ShapeDtypeStruct((8, slots), F32),
            jax.ShapeDtypeStruct((vocab_rows, resp), BF16),
            jax.ShapeDtypeStruct((resp, width), BF16),
            jax.ShapeDtypeStruct(hidden.shape, BF16),
            jax.ShapeDtypeStruct((1, 1), F32),
        ),
        in_specs=[vmem] * 8 + [hbm],
        out_specs=(hbm, hbm, vmem, vmem, vmem, vmem, vmem),
        scratch_shapes=[
            pltpu.VMEM((vocab_rows, width), BF16),
            pltpu.VMEM((slots, packed_width), BF16),
            pltpu.VMEM((ROWS, half), BF16),
            pltpu.VMEM((seq * ROWS, half), BF16),
            pltpu.VMEM((vocab_rows, resp), F32),
            pltpu.VMEM((n, 8, resp), F32),
            pltpu.VMEM((n, 8, resp), F32),
            pltpu.VMEM((resp, width), F32),
            pltpu.VMEM((seq, resp // seq, width), F32),
            pltpu.VMEM((tensor, resp // seq, slab), F32),
            pltpu.VMEM((tensor, resp // seq, slab), F32),
            pltpu.VMEM((resp // seq, slab), F32),
            pltpu.VMEM((tensor, resp // seq, slab), F32),
            pltpu.SemaphoreType.DMA,
            pltpu.SemaphoreType.DMA,
            pltpu.SemaphoreType.DMA((TOKENS + WAVES,)),
            pltpu.SemaphoreType.DMA((TOKENS + WAVES,)),
        ]
        + (early_scratch if early_waves else []),
        compiler_params=pltpu.CompilerParams(
            collective_id=0, has_side_effects=True, vmem_limit_bytes=60 << 20
        ),
        name="exchange",
    )(
        targets.reshape(1, resp),
        branch.reshape(1, resp),
        pair_of_row.reshape(1, resp),
        ref_log_prob.reshape(1, resp),
        pair_weight.reshape(1, pairs),
        token_ids.reshape(1, tokens),
        hidden,
        token_grad,
        weight,
    )
    last = parts * subs - 1
    weight_grad = pl.pallas_call(
        functools.partial(weight_grad_kernel, capacity, parts, subs, skipped, norm),
        grid=(steps,),
        out_shape=jax.ShapeDtypeStruct(weight.shape, BF16),
        in_specs=[
            pl.BlockSpec((slots - skipped, block), lambda i: (0, jnp.minimum(i, last))),
            pl.BlockSpec((8, slots), lambda i: (0, 0)),
            pl.BlockSpec((vocab_rows, resp), lambda i: (0, 0)),
            pl.BlockSpec((resp, block), lambda i: (0, i)),
            pl.BlockSpec((1,) + base_shape[1:], lambda i: (jnp.minimum(i, base_shape[0] - 1), 0, 0)),
        ],
        out_specs=pl.BlockSpec((vocab_rows, block), lambda i: (0, i)),
        scratch_shapes=[
            pltpu.VMEM((vocab_rows, slots - skipped), BF16),
            pltpu.VMEM((subs, slots - skipped, block), BF16),
        ],
        compiler_params=pltpu.CompilerParams(vmem_limit_bytes=56 << 20),
        name="weight_grad",
    )(arrived, tags, dlogits, gathered, base)
    return (loss.reshape(()), weight_grad, hidden_grad)


def solution(mesh):
    return jax.shard_map(
        shards,
        mesh=mesh,
        in_specs=(
            P(("seq", "tensor"), None),
            P("seq", None),
            P(),
            P(),
            P(),
            P(),
            P(),
            P(("seq", "tensor")),
            P(("seq", "tensor"), None),
        ),
        out_specs=(P(), P(("seq", "tensor"), None), P("seq", None)),
        check_vma=False,
    )
```

```python
import functools
import math

import jax
import jax.numpy as jnp
from jax import lax
from jax.experimental import pallas as pl
from jax.experimental.pallas import tpu as pltpu
from jax.sharding import PartitionSpec as P

dpo_beta = 0.1
LANES = 128
ROWS = 16
CHUNK = 128
TOKENS = 7
WAVES = 4
MESH = pl.DeviceIdType.MESH
F32, BF16 = jnp.float32, jnp.bfloat16


def pack_plan(capacity, tiles):
    for piece in range(tiles // 2, 0, -1):
        parts = tiles // piece - 1
        if tiles % piece == 0 and (ROWS - capacity) * parts >= capacity:
            return piece, parts
    raise ValueError("no packing")


def unpack_pick(capacity, parts, part):
    to = lax.broadcasted_iota(jnp.int32, (CHUNK, CHUNK), 0)
    source = lax.broadcasted_iota(jnp.int32, (CHUNK, CHUNK), 1)
    bits = ROWS.bit_length() - 1
    spare = (source & (ROWS - 1)) - capacity
    chosen = (
        (jnp.right_shift(to, bits) == jnp.right_shift(source, bits))
        & (spare >= 0)
        & ((to & (ROWS - 1)) == spare * parts + part)
    )
    return jnp.where(chosen, 1.0, 0.0).astype(BF16)


def exchange_kernel(
    seq, tensor, capacity, piece, parts, block, early_waves, norm,
    targets, branch, pair_of_row, ref_log_prob, pair_weight_row, ids_row, hidden_rows, token_grad, weight_hbm,
    arrived, base_hbm, tags, dlogits, gathered, hidden_grad, loss,
    weight, packed, hidden, folded, logits, stat, stats, partial, seq_parts, sums, tensor_parts, done, pieces,
    load_sem, own_sem, send_sems, recv_sems, *early_scratch,
):
    n = seq * tensor
    vocab_rows, width = weight.shape
    resp = targets.shape[1]
    tokens = ids_row.shape[1]
    mine_seq, mine_tensor = lax.axis_index("seq"), lax.axis_index("tensor")
    me = mine_seq * tensor + mine_tensor

    core = lax.rem(mine_seq, 2)

    def exclusive_or(a, b, size):
        total = 0
        for bit in [1 << k for k in range(size.bit_length() - 1)]:
            total = total + lax.rem(lax.div(a, bit) + lax.div(b, bit), 2) * bit
        return total

    own_block = 1 - core

    def device(b):
        place = lax.rem(b, tensor)
        bits = lax.rem(place + 1 + core, 2) * (tensor // 2) + lax.div(place, 2)
        return (
            exclusive_or(mine_seq, lax.div(b, tensor), seq),
            exclusive_or(mine_tensor, bits, tensor),
        )

    def send(src, dst, kind, target):
        pltpu.make_async_remote_copy(
            src_ref=src, dst_ref=dst, send_sem=send_sems.at[kind], recv_sem=recv_sems.at[kind],
            device_id=target, device_id_type=MESH,
        ).start()

    def wait(sems, kind, ref):
        pltpu.make_async_copy(ref, ref, sems.at[kind]).wait()

    load = pltpu.make_async_copy(weight_hbm, weight, load_sem)
    load.start()
    half = width // 2
    whole = hidden_rows[...].astype(F32)
    hidden[...] = jnp.concatenate([whole[:, :half], whole[:, half:]], axis=0).astype(BF16)
    folded[pl.ds(pl.multiple_of(mine_seq * ROWS, ROWS), ROWS)] = hidden[...]
    barrier = pltpu.get_barrier_semaphore()

    def greet(rel, carry):
        peer = lax.rem(me + rel, n)
        pl.semaphore_signal(
            barrier, inc=1, device_id=(lax.div(peer, tensor), lax.rem(peer, tensor)), device_id_type=MESH
        )
        return carry

    lax.fori_loop(1, n, greet, 0)

    shift = vocab_rows.bit_length() - 1
    owner = jnp.right_shift(ids_row[...], shift)
    before = lax.broadcasted_iota(jnp.int32, (tokens, tokens), 0) < lax.broadcasted_iota(
        jnp.int32, (tokens, tokens), 1
    )
    to_owner = lax.broadcasted_iota(jnp.int32, (n, tokens), 0) == owner
    earlier = jnp.dot(
        jnp.where(to_owner, 1.0, 0.0).astype(BF16),
        jnp.where(before, 1.0, 0.0).astype(BF16),
        preferred_element_type=F32,
    )
    slot = jnp.sum(jnp.where(to_owner, earlier, 0.0), axis=0, keepdims=True).astype(jnp.int32)
    seq_bits = jnp.right_shift(owner, tensor.bit_length() - 1) ^ mine_seq
    tensor_bits = (owner & (tensor - 1)) ^ mine_tensor
    crosses = jnp.where(tensor_bits >= tensor // 2, 1, 0)
    rel_owner = seq_bits * tensor + (tensor_bits & (tensor // 2 - 1)) * 2 + ((crosses + 1 + core) & 1)
    spare = jnp.zeros_like(slot)
    for j in range(1, ROWS - capacity):
        spare = spare + jnp.where(slot >= j * parts, 1, 0)
    part_of = slot - spare * parts
    main_row = rel_owner * ROWS + slot
    spare_row = rel_owner * ROWS + capacity + spare
    label = (ids_row[...] - owner * vocab_rows + 1).astype(F32)
    piece_width = piece * LANES
    chunks = n * ROWS // CHUNK
    wave_rows = n * ROWS // WAVES
    if early_waves:
        early, base, rest, base_sems = early_scratch

    def exact_dot(left, right, dims):
        high = left.astype(BF16)
        low = (left - high.astype(F32)).astype(BF16)
        ones = right.astype(BF16)
        return lax.dot_general(high, ones, dims, preferred_element_type=F32) + lax.dot_general(
            low, ones, dims, preferred_element_type=F32
        )

    to_rel = lax.broadcasted_iota(jnp.int32, (n, tokens), 0) == rel_owner
    at_slot = jnp.where(lax.broadcasted_iota(jnp.int32, (resp, tokens), 0) == slot, 1.0, 0.0)
    stat[...] = jnp.zeros_like(stat)
    stat[:, 3, :] = exact_dot(jnp.where(to_rel, label, 0.0), at_slot, (((1,), (1,)), ((), ())))

    pl.semaphore_wait(barrier, n - 1)

    mine_rows = pl.ds(pl.multiple_of(mine_seq * ROWS, ROWS), ROWS)
    for k in range(1, seq):
        send(hidden, folded.at[mine_rows], 0, (lax.rem(mine_seq + k, seq), mine_tensor))

    def pack(wave, chunk, carry):
        first = pl.multiple_of(chunk * CHUNK, CHUNK)
        rows = first + lax.broadcasted_iota(jnp.int32, (CHUNK, tokens), 0)
        main = rows == main_row
        in_spare = rows == spare_row
        main_pick = jnp.where(main, 1.0, 0.0).astype(BF16)
        for part in range(parts):
            last = in_spare & (part_of == part)
            last_pick = jnp.where(last, 1.0, 0.0).astype(BF16)
            here = pl.ds(part * piece_width, piece_width)
            packed[pl.ds(first, CHUNK), here] = (
                jnp.dot(main_pick, token_grad[:, here], preferred_element_type=F32)
                + jnp.dot(
                    last_pick, token_grad[:, parts * piece_width :], preferred_element_type=F32
                )
            ).astype(BF16)

        return carry

    def pack_wave(wave):
        lax.fori_loop(wave * chunks // WAVES, (wave + 1) * chunks // WAVES, functools.partial(pack, wave), 0)

    def send_blocks(first_eighth, end_eighth):
        for eighth in range(first_eighth, end_eighth):
            wave = eighth * WAVES // 8

            def send_block(b, carry):
                src = pl.ds(pl.multiple_of(b * ROWS, ROWS), ROWS)
                if wave < early_waves:
                    land = early.at[src]
                else:
                    land = arrived.at[pl.ds(pl.multiple_of(b * ROWS - early_waves * wave_rows, ROWS), ROWS)]

                @pl.when(b != own_block)
                def _():
                    send(packed.at[src], land, TOKENS + wave, device(b))

                return carry

            lax.fori_loop(eighth * n // 8, (eighth + 1) * n // 8, send_block, 0)

    pack_wave(0)
    send_blocks(0, 2)
    pack_wave(1)
    own_rows = pl.ds(pl.multiple_of(own_block * ROWS, ROWS), ROWS)
    own = pltpu.make_async_copy(packed.at[own_rows], (early if early_waves else arrived).at[own_rows], own_sem)
    own.start()

    wait(recv_sems, 0, folded.at[pl.ds(0, (seq - 1) * ROWS)])
    for pair in range(seq // 2):
        both = folded[pair * 2 * ROWS : (pair + 1) * 2 * ROWS].astype(F32)
        rows = pl.ds(pair * ROWS, ROWS)
        gathered[rows, :half] = jnp.concatenate([both[0:8], both[16:24]], axis=0).astype(BF16)
        gathered[rows, half:] = jnp.concatenate([both[8:16], both[24:32]], axis=0).astype(BF16)
    load.wait()
    step = 6 * LANES
    logits[...] = jnp.zeros_like(logits)

    def add_logits(i, carry):
        columns = pl.ds(pl.multiple_of(i * step, step), step)
        logits[...] += lax.dot_general(
            weight[:, columns], gathered[:, columns], (((1,), (1,)), ((), ())), preferred_element_type=F32
        )
        return carry

    lax.fori_loop(0, width // step, add_logits, 0)
    value = logits[...]
    top = jnp.max(value, axis=0, keepdims=True)
    hit = lax.broadcasted_iota(jnp.int32, (vocab_rows, resp), 0) == targets[...] - me * vocab_rows
    stat[:, 0, :] = jnp.broadcast_to(top, (n, resp))
    stat[:, 1, :] = jnp.broadcast_to(jnp.sum(jnp.exp(value - top), axis=0, keepdims=True), (n, resp))
    stat[:, 2, :] = jnp.broadcast_to(jnp.sum(jnp.where(hit, value, 0.0), axis=0, keepdims=True), (n, resp))
    stats[pl.ds(me, 1)] = stat[pl.ds(own_block, 1)]

    def send_stat(rel, carry):
        @pl.when(rel != own_block)
        def _():
            send(stat.at[rel], stats.at[me], 3, device(rel))

        return carry

    lax.fori_loop(0, n, send_stat, 0)
    send_blocks(2, 3)
    pack_wave(2)
    wait(recv_sems, 3, stats.at[pl.ds(0, n - 1)])
    tops = stats[:, 0, :]
    row_top = jnp.max(tops, axis=0, keepdims=True)
    row_total = jnp.sum(jnp.exp(tops - row_top) * stats[:, 1, :], axis=0, keepdims=True)
    target_logit = jnp.sum(stats[:, 2, :], axis=0, keepdims=True)
    log_prob = target_logit - row_top - jnp.log(row_total)
    sign = jnp.where(branch[...] == 1, 1.0, 0.0) - jnp.where(branch[...] == 2, 1.0, 0.0)
    pairs = pair_weight_row.shape[1]
    same = lax.broadcasted_iota(jnp.int32, (pairs, pairs), 0) == lax.broadcasted_iota(
        jnp.int32, (pairs, pairs), 1
    )
    pair_weight = jnp.sum(jnp.where(same, pair_weight_row[...], 0.0), axis=1, keepdims=True)
    member = lax.broadcasted_iota(jnp.int32, (pairs, resp), 0) == pair_of_row[...]
    margin = jnp.sum(jnp.where(member, sign * (log_prob - ref_log_prob[...]), 0.0), axis=1, keepdims=True)
    z = -dpo_beta * margin
    softplus = jnp.maximum(z, 0.0) + jnp.log1p(jnp.exp(-jnp.abs(z)))
    loss[...] = jnp.sum(pair_weight * softplus, axis=0, keepdims=True)
    push_back = pair_weight * lax.logistic(z)
    row_scale = -dpo_beta * sign * jnp.sum(jnp.where(member, push_back, 0.0), axis=0, keepdims=True)
    probs = jnp.exp(value - row_top) / row_total
    rounded = (row_scale * (jnp.where(hit, 1.0, 0.0) - probs)).astype(BF16)
    dlogits[...] = rounded
    by_row = jnp.transpose(rounded.astype(F32)).astype(BF16)

    def add_partial(i, carry):
        columns = pl.ds(pl.multiple_of(i * step, step), step)
        partial[:, columns] = jnp.dot(by_row, weight[:, columns], preferred_element_type=F32)
        return carry

    lax.fori_loop(0, width // step, add_partial, 0)
    share = resp // seq
    for k in range(1, seq):
        peer = lax.rem(mine_seq + k, seq)
        rows = pl.ds(pl.multiple_of(peer * share, share), share)
        send(partial.at[rows], seq_parts.at[mine_seq], 4, (peer, mine_tensor))
    send_blocks(3, 5)
    pack_wave(3)
    rows = pl.ds(pl.multiple_of(mine_seq * share, share), share)
    seq_parts[pl.ds(mine_seq, 1)] = partial[rows, :][None]
    wait(recv_sems, 4, seq_parts.at[pl.ds(0, seq - 1)])
    total = seq_parts[0]
    for k in range(1, seq):
        total = total + seq_parts[k]
    slab = sums.shape[2]
    cuts = [(i, i * slab, min((i + 1) * slab, width)) for i in range(tensor) if i * slab < width]
    sums[...] = jnp.zeros_like(sums)
    for i, low, high in cuts:
        sums[i, :, : high - low] = total[:, low:high]
    for k in range(1, tensor):
        peer = lax.rem(mine_tensor + k, tensor)
        send(sums.at[peer], tensor_parts.at[mine_tensor], 5, (mine_seq, peer))
    send_blocks(5, 6)
    tensor_parts[pl.ds(mine_tensor, 1)] = sums[pl.ds(mine_tensor, 1)]
    wait(recv_sems, 5, tensor_parts.at[pl.ds(0, tensor - 1)])
    total = tensor_parts[0]
    for k in range(1, tensor):
        total = total + tensor_parts[k]
    done[...] = total
    pieces[pl.ds(mine_tensor, 1)] = total[None]
    for k in range(1, tensor):
        send(done, pieces.at[mine_tensor], 6, (mine_seq, lax.rem(mine_tensor + k, tensor)))
    send_blocks(6, 8)

    slots = n * ROWS
    column = lax.broadcasted_iota(jnp.int32, (resp, slots), 1)
    column = column - jnp.right_shift(column, ROWS.bit_length() - 1) * ROWS
    wanted = lax.broadcasted_iota(jnp.int32, (resp, slots), 0)
    came = lax.broadcasted_iota(jnp.int32, (n, slots), 1)
    came = jnp.right_shift(came, ROWS.bit_length() - 1)
    place = came & (tensor - 1)
    seq_bits = jnp.right_shift(came, tensor.bit_length() - 1)
    crosses = (place + 1 + ((seq_bits + core) & 1)) & 1
    tensor_bits = crosses * (tensor // 2) + jnp.right_shift(place, 1)
    came = (seq_bits ^ mine_seq) * tensor + (tensor_bits ^ mine_tensor)
    came = came == lax.broadcasted_iota(jnp.int32, (n, slots), 0)
    sent_labels = stats[:, 3, :]
    tags[...] = jnp.zeros_like(tags)
    chosen = (column == wanted) & (column < capacity)
    spread = exact_dot(sent_labels, jnp.where(chosen, 1.0, 0.0), (((1,), (0,)), ((), ())))
    tags[0:1, :] = jnp.sum(jnp.where(came, spread, 0.0), axis=0, keepdims=True)

    own.wait()

    def wait_wave(wave):
        low, high = wave * wave_rows + (ROWS if wave == 0 else 0), (wave + 1) * wave_rows
        wait(send_sems, TOKENS + wave, packed.at[pl.ds(low, high - low)])
        if wave < early_waves:
            wait(recv_sems, TOKENS + wave, early.at[pl.ds(low, high - low)])
        else:
            wait(recv_sems, TOKENS + wave, arrived.at[pl.ds(low - early_waves * wave_rows, high - low)])

    if early_waves:
        for wave in range(early_waves):
            wait_wave(wave)
        count = early_waves * wave_rows
        vocab = lax.broadcasted_iota(jnp.int32, (vocab_rows, count), 0).astype(F32) + 1.0
        main_pick = jnp.where(vocab == tags[0:1, :count], 1.0, 0.0).astype(BF16)
        subs = piece_width // block
        picks = [unpack_pick(capacity, parts, part) for part in range(parts)]
        for sub in range(subs):
            for low in range(0, count, CHUNK):
                last = jnp.zeros((CHUNK, block), F32)
                for part in range(parts):
                    here = pl.ds((part * subs + sub) * block, block)
                    last = last + jnp.dot(picks[part], early[low : low + CHUNK, here], preferred_element_type=F32)
                rest[sub, low : low + CHUNK, :] = last.astype(BF16)
        stores = []
        for i in range((parts + 1) * subs):
            here = pl.ds(i * block, block)
            rows = early[:, here] if i < parts * subs else rest[i % subs]
            head = jnp.dot(dlogits[...], gathered[:, here], preferred_element_type=F32)
            base[i] = head + norm * jnp.dot(main_pick, rows, preferred_element_type=F32)
            stores.append(pltpu.make_async_copy(base.at[i], base_hbm.at[i], base_sems.at[i]))
            stores[-1].start()
        for store in stores:
            store.wait()
    wait(recv_sems, 6, pieces.at[pl.ds(0, tensor - 1)])
    for i, low, high in cuts:
        hidden_grad[:, low:high] = pieces[i, :, : high - low].astype(BF16)

    for wave in range(early_waves, WAVES):
        wait_wave(wave)
    wait(send_sems, 0, folded.at[pl.ds(0, (seq - 1) * ROWS)])
    wait(send_sems, 3, stats.at[pl.ds(0, n - 1)])
    wait(send_sems, 4, seq_parts.at[pl.ds(0, seq - 1)])
    wait(send_sems, 5, tensor_parts.at[pl.ds(0, tensor - 1)])
    wait(send_sems, 6, pieces.at[pl.ds(0, tensor - 1)])


def weight_grad_kernel(capacity, parts, subs, skipped, norm, arrived, tags, dlogits, gathered, base, out, main_pick, rest):
    i = pl.program_id(0)
    vocab_rows, slots = main_pick.shape
    vocab = lax.broadcasted_iota(jnp.int32, (vocab_rows, slots), 0).astype(F32) + 1.0

    @pl.when(i == 0)
    def _():
        main_pick[...] = jnp.where(vocab == tags[0:1, skipped:], 1.0, 0.0).astype(BF16)
        rest[...] = jnp.zeros_like(rest)

    if skipped:
        before = base[0]
    else:
        before = jnp.dot(dlogits[...], gathered[...], preferred_element_type=F32)
    sub = lax.rem(i, subs)

    def store(rows):
        out[...] = (before + norm * jnp.dot(main_pick[...], rows, preferred_element_type=F32)).astype(BF16)

    @pl.when(i < parts * subs)
    def _():
        store(arrived[...])
        pick = unpack_pick(capacity, parts, lax.div(i, subs))

        def unpack(chunk, carry):
            rows = pl.ds(pl.multiple_of(chunk * CHUNK, CHUNK), CHUNK)
            moved = jnp.dot(pick, arrived[rows, :], preferred_element_type=F32)
            rest[sub, rows, :] = (rest[sub, rows, :].astype(F32) + moved).astype(BF16)
            return carry

        lax.fori_loop(0, slots // CHUNK, unpack, 0)

    @pl.when(i >= parts * subs)
    def _():
        store(rest[sub])


def shards(
    weight, hidden, targets, branch, pair_of_row, ref_log_prob, pair_weight, token_ids, token_grad
):
    vocab_rows, width = weight.shape
    seq, tensor = lax.axis_size("seq"), lax.axis_size("tensor")
    n = seq * tensor
    resp, tokens, pairs = targets.shape[0], token_ids.shape[0], pair_weight.shape[0]
    capacity = max(2, (2 * tokens + n - 1) // n)
    tiles = width // LANES
    piece, parts = pack_plan(capacity, tiles)
    subs = next(k for k in range(1, piece + 1) if piece % k == 0 and piece // k <= 8)
    block = piece // subs * LANES
    packed_width = parts * piece * LANES
    slab = (tiles + tensor - 1) // tensor * LANES
    half = width // 2
    vmem, hbm = pl.BlockSpec(memory_space=pltpu.VMEM), pl.BlockSpec(memory_space=pl.ANY)
    norm = math.sqrt(width)
    slots = n * ROWS
    early_waves = WAVES - 1 if slots * packed_width * 2 <= 8 << 20 else 0
    skipped = early_waves * slots // WAVES
    steps = (parts + 1) * subs
    base_shape = (steps, vocab_rows, block) if early_waves else (1, 8, LANES)
    early_scratch = [
        pltpu.VMEM((skipped, packed_width), BF16),
        pltpu.VMEM(base_shape, F32),
        pltpu.VMEM((subs, skipped, block), BF16),
        pltpu.SemaphoreType.DMA((steps,)),
    ]
    arrived, base, tags, dlogits, gathered, hidden_grad, loss = pl.pallas_call(
        functools.partial(exchange_kernel, seq, tensor, capacity, piece, parts, block, early_waves, norm),
        out_shape=(
            jax.ShapeDtypeStruct((slots - skipped, packed_width), BF16),
            jax.ShapeDtypeStruct(base_shape, F32),
            jax.ShapeDtypeStruct((8, slots), F32),
            jax.ShapeDtypeStruct((vocab_rows, resp), BF16),
            jax.ShapeDtypeStruct((resp, width), BF16),
            jax.ShapeDtypeStruct(hidden.shape, BF16),
            jax.ShapeDtypeStruct((1, 1), F32),
        ),
        in_specs=[vmem] * 8 + [hbm],
        out_specs=(hbm, hbm, vmem, vmem, vmem, vmem, vmem),
        scratch_shapes=[
            pltpu.VMEM((vocab_rows, width), BF16),
            pltpu.VMEM((slots, packed_width), BF16),
            pltpu.VMEM((ROWS, half), BF16),
            pltpu.VMEM((seq * ROWS, half), BF16),
            pltpu.VMEM((vocab_rows, resp), F32),
            pltpu.VMEM((n, 8, resp), F32),
            pltpu.VMEM((n, 8, resp), F32),
            pltpu.VMEM((resp, width), F32),
            pltpu.VMEM((seq, resp // seq, width), F32),
            pltpu.VMEM((tensor, resp // seq, slab), F32),
            pltpu.VMEM((tensor, resp // seq, slab), F32),
            pltpu.VMEM((resp // seq, slab), F32),
            pltpu.VMEM((tensor, resp // seq, slab), F32),
            pltpu.SemaphoreType.DMA,
            pltpu.SemaphoreType.DMA,
            pltpu.SemaphoreType.DMA((TOKENS + WAVES,)),
            pltpu.SemaphoreType.DMA((TOKENS + WAVES,)),
        ]
        + (early_scratch if early_waves else []),
        compiler_params=pltpu.CompilerParams(
            collective_id=0, has_side_effects=True, vmem_limit_bytes=60 << 20
        ),
        name="exchange",
    )(
        targets.reshape(1, resp),
        branch.reshape(1, resp),
        pair_of_row.reshape(1, resp),
        ref_log_prob.reshape(1, resp),
        pair_weight.reshape(1, pairs),
        token_ids.reshape(1, tokens),
        hidden,
        token_grad,
        weight,
    )
    last = parts * subs - 1
    weight_grad = pl.pallas_call(
        functools.partial(weight_grad_kernel, capacity, parts, subs, skipped, norm),
        grid=(steps,),
        out_shape=jax.ShapeDtypeStruct(weight.shape, BF16),
        in_specs=[
            pl.BlockSpec((slots - skipped, block), lambda i: (0, jnp.minimum(i, last))),
            pl.BlockSpec((8, slots), lambda i: (0, 0)),
            pl.BlockSpec((vocab_rows, resp), lambda i: (0, 0)),
            pl.BlockSpec((resp, block), lambda i: (0, i)),
            pl.BlockSpec((1,) + base_shape[1:], lambda i: (jnp.minimum(i, base_shape[0] - 1), 0, 0)),
        ],
        out_specs=pl.BlockSpec((vocab_rows, block), lambda i: (0, i)),
        scratch_shapes=[
            pltpu.VMEM((vocab_rows, slots - skipped), BF16),
            pltpu.VMEM((subs, slots - skipped, block), BF16),
        ],
        compiler_params=pltpu.CompilerParams(vmem_limit_bytes=56 << 20),
        name="weight_grad",
    )(arrived, tags, dlogits, gathered, base)
    return (loss.reshape(()), weight_grad, hidden_grad)


def solution(mesh):
    return jax.shard_map(
        shards,
        mesh=mesh,
        in_specs=(
            P(("seq", "tensor"), None),
            P("seq", None),
            P(),
            P(),
            P(),
            P(),
            P(),
            P(("seq", "tensor")),
            P(("seq", "tensor"), None),
        ),
        out_specs=(P(), P(("seq", "tensor"), None), P("seq", None)),
        check_vma=False,
    )
```
